256 devices in a mesh: inst: 64 (over z, x, core), tp: 4 (over y).
Axes of the slice: x: 4, y: 4, z: 8, core: 2. Of those that a mesh axis runs over, the one named last changes fastest.
Arguments:
- queries: bfloat16 [512, 64, 128], P('inst', 'tp'), may hold values from -8 to 8
- keys_cache: bfloat16 [9856, 8, 64, 128], P('inst', 'tp'), may hold values from -12 to 12
- value_block_cache: bfloat16 [9856, 8, 64, 128], P('inst', 'tp'), may hold values from -6 to 6
- block_table: int32 [512, 48], P('inst'), may hold values from -1 to 9855, as said below
- ctx_len: int32 [512], P('inst'), may hold values from 1 to 3072, as said below
- out_weight: bfloat16 [8192, 8192], P('tp', 'inst'), may hold values from -0.25 to 0.25
Outputs:
- mixed: bfloat16 [512, 8192], P('tp', 'inst')
The draws below stay inside these ranges and needn't reach their ends.
Inputs may be any that keep to these rules, and one draw needn't show every extreme that they name: `block_table`: row n lists the blocks of request n for b < ceil(ctx_len[n] / 64) as j * 154 + page, where j is the instance that holds the block, and -1 after them; no block is listed twice. The blocks of the request of instance h that spans 48 blocks lie on instances j other than h, at page 28 + (((j - h) mod 64) - 1) * 2 + c with 0 <= c < 2; the blocks of its other requests lie on h itself, at pages below 28. `ctx_len`: on each instance one request spans 48 blocks, another exactly 4, and every other one at most 4.
All inputs are finite; a program needn't handle non-finite values.
Results may differ from the reference program's by a relative error of at most 0.0051.
Values may be sent and summed in bfloat16 or wider, within the bound.
A program may use at most 64 MiB of HBM per device.

```python
import math
import jax
import jax.numpy as jnp
from jax import lax

D = 8192
QUERY_HEADS = 64
KEY_VALUE_HEADS = 8
HEAD_SIZE = 128
R = 8
BLOCK_TOKENS = 64
CAP = 2
MAXB = 48
OTHERB = 4
INSTANCE_BLOCKS = 154
N_INST = 64


def layout(key):
    start_key = jax.random.fold_in(key, 77)
    key_long, key_other, key_tail, key_perm, key_first, key_home = jax.random.split(start_key, 6)
    lent_total = CAP * (N_INST - 1)
    home_total = (R - 1) * OTHERB
    longest = jax.random.randint(key_long, (N_INST, 1), 0, R)
    request_ids = jnp.arange(R, dtype=jnp.int32)[None, :]
    is_long = request_ids == longest
    is_full = request_ids == (longest + 1) % R
    other_len = jax.random.randint(key_other, (N_INST, R), 1, OTHERB + 1)
    blocks = jnp.where(is_long, MAXB, jnp.where(is_full, OTHERB, other_len))
    tail_tokens = jax.random.randint(key_tail, (N_INST, R), 1, BLOCK_TOKENS + 1)
    home_ids = jnp.arange(N_INST, dtype=jnp.int32)[:, None]
    tail_tokens = jnp.where(is_long & (home_ids == 0), BLOCK_TOKENS, tail_tokens)
    lengths = (blocks - 1) * BLOCK_TOKENS + tail_tokens
    rest_blocks = jnp.where(is_long, 0, blocks)
    before = jnp.cumsum(rest_blocks, axis=1) - rest_blocks

    def shuffle_lent(one_key):
        return jax.random.permutation(one_key, lent_total)

    def shuffle_home(one_key):
        return jax.random.permutation(one_key, home_total)
    lent_perm = jax.vmap(shuffle_lent)(jax.random.split(key_perm, N_INST)).astype(jnp.int32)
    first_home = jnp.concatenate([jnp.array([lent_total - 1], dtype=jnp.int32), jax.random.permutation(key_first, lent_total - 1).astype(jnp.int32)])
    lent_perm = lent_perm.at[0].set(first_home)
    home_perm = jax.vmap(shuffle_home)(jax.random.split(key_home, N_INST)).astype(jnp.int32)
    block_ids = jnp.arange(MAXB, dtype=jnp.int32)
    home_three = jnp.arange(N_INST, dtype=jnp.int32)[:, None, None]
    in_use = block_ids[None, None, :] < blocks[:, :, None]
    home_pos = jnp.minimum(before[:, :, None] + block_ids[None, None, :], home_total - 1)
    home_slot = home_perm[home_three, home_pos]
    home_page = home_three * INSTANCE_BLOCKS + home_slot
    lent_slot = lent_perm[:, jnp.minimum(block_ids, lent_total - 1)]
    offset = lent_slot // CAP + 1
    within = lent_slot % CAP
    lender = (jnp.arange(N_INST, dtype=jnp.int32)[:, None] + offset) % N_INST
    lent_page = lender * INSTANCE_BLOCKS + home_total + (offset - 1) * CAP + within
    page_ids = jnp.where(is_long[:, :, None], lent_page[:, None, :], home_page)
    table_rows = jnp.where(in_use, page_ids, -1).reshape(N_INST * R, MAXB)
    return (table_rows.astype(jnp.int32), lengths.reshape(N_INST * R).astype(jnp.int32))


def draw_block_table(key, part):
    table_rows, lengths = layout(key)
    return table_rows


def draw_ctx_len(key, part):
    table_rows, lengths = layout(key)
    return lengths


def draw_queries(key, part):
    key = jax.random.fold_in(key, 5)
    key_base = jax.random.fold_in(key, 0)
    every_dimension = (N_INST * R, QUERY_HEADS, HEAD_SIZE)
    result = jnp.clip(2.0 * jax.random.normal(key_base, every_dimension, jnp.float32), -8.0, 8.0)
    return result.astype(jnp.bfloat16)


def draw_keys_cache(key, part):
    key = jax.random.fold_in(key, 6)
    key_base = jax.random.fold_in(key, 0)
    block_grand_total = N_INST * INSTANCE_BLOCKS
    every_dimension = (block_grand_total, KEY_VALUE_HEADS, BLOCK_TOKENS, HEAD_SIZE)
    result = jnp.clip(jax.random.normal(key_base, every_dimension, jnp.float32), -4.5, 4.5)
    return result.astype(jnp.bfloat16)


def levels(stream_key, shape, pieces, least, largest):
    gain = 1.0
    for position, shards_of in pieces:
        steps = jax.random.uniform(jax.random.fold_in(jax.random.fold_in(stream_key, 6), position), (shards_of,), jnp.float32, least / len(pieces), largest / len(pieces))
        gain = gain * jnp.repeat(jnp.exp(steps), shape[position] // shards_of).reshape((-1,) + (1,) * (len(shape) - 1 - position))
    return gain


def scatter_about(own_key, extent, scale, reach, shards=(), kind=jnp.bfloat16):
    gain = levels(own_key, extent, shards, -0.22, 0.18) if shards else 1.0
    values = jax.random.normal(own_key, extent, jnp.float32) * scale * gain
    return jnp.minimum(jnp.maximum(values, -reach), reach).astype(kind)


def setup_inputs(seed: int = 0) -> dict:
    seeds = jax.random.split(jax.random.key(seed), 7)
    queries = draw_queries(jax.random.fold_in(seeds[6], 71), 0)
    keys_cache = draw_keys_cache(jax.random.fold_in(seeds[6], 71), 0)
    value_block_cache = scatter_about(seeds[2], (N_INST * INSTANCE_BLOCKS, KEY_VALUE_HEADS, BLOCK_TOKENS, HEAD_SIZE), 1.0, 6.0, ((0, 64), (1, 4)))
    block_table = draw_block_table(jax.random.fold_in(seeds[6], 71), 0)
    ctx_len = draw_ctx_len(jax.random.fold_in(seeds[6], 71), 0)
    out_weight = scatter_about(seeds[5], (QUERY_HEADS * HEAD_SIZE, D), (QUERY_HEADS * HEAD_SIZE // 16) ** -0.5, 0.25, ((0, 4), (1, 64)))
    return {"queries": queries, "keys_cache": keys_cache, "value_block_cache": value_block_cache, "block_table": block_table, "ctx_len": ctx_len, "out_weight": out_weight}


very_low = -1e+30

def reference(queries, keys_cache, value_block_cache, block_table, ctx_len, out_weight):
    query_group_width = QUERY_HEADS // KEY_VALUE_HEADS
    scaling = 1.0 / math.sqrt(HEAD_SIZE)
    block_ids = jnp.arange(MAXB, dtype=jnp.int32)
    token_ids = jnp.arange(BLOCK_TOKENS, dtype=jnp.int32)

    def per_request(request_items):
        single_query, table_row, length = request_items
        valid_tokens = jnp.clip(length - block_ids * BLOCK_TOKENS, 0, BLOCK_TOKENS).astype(jnp.int32)
        page_rows = jnp.where(valid_tokens > 0, table_row, 0).astype(jnp.int32)
        key_rows = keys_cache[page_rows].astype(jnp.float32)
        value_rows = value_block_cache[page_rows].astype(jnp.float32)
        query_groups = single_query.reshape(KEY_VALUE_HEADS, query_group_width, HEAD_SIZE).astype(jnp.float32)
        scores = jnp.einsum('kgd,bktd->bkgt', query_groups, key_rows, precision=lax.Precision.HIGHEST) * scaling
        live_mask = (token_ids[None, :] < valid_tokens[:, None])[:, None, None, :]
        block_top = lax.optimization_barrier(jnp.max(jnp.where(live_mask, scores, very_low), axis=-1))
        raised = jnp.where(live_mask, jnp.exp(scores - block_top[..., None]), 0.0)
        block_total = lax.optimization_barrier(jnp.sum(raised, axis=-1))
        rounded = lax.optimization_barrier(raised.astype(jnp.bfloat16))
        weights = rounded.astype(jnp.float32)
        block_out = jnp.einsum('bkgt,bktd->bkgd', weights, value_rows, precision=lax.Precision.HIGHEST)
        overall = lax.optimization_barrier(jnp.max(block_top, axis=0))
        factors = jnp.exp(block_top - overall)
        numerator = lax.optimization_barrier(jnp.sum(factors[..., None] * block_out, axis=0))
        denominator = lax.optimization_barrier(jnp.sum(factors * block_total, axis=0))
        return (numerator / denominator[..., None]).astype(jnp.bfloat16).reshape(QUERY_HEADS * HEAD_SIZE)
    attention = lax.map(per_request, (queries, block_table, ctx_len))
    return jnp.dot(attention, out_weight, preferred_element_type=jnp.float32).astype(jnp.bfloat16)
```

```python
import math

import jax
import jax.numpy as jnp
from jax import lax
from jax.experimental import pallas as pl
from jax.experimental.pallas import tpu as pltpu
from jax.sharding import PartitionSpec as P

MESH = pl.DeviceIdType.MESH
F32 = jnp.float32
BF16 = jnp.bfloat16

N_INST = 64
TP = 4
ZN, XN = 8, 4
R = 8
HEADS = 16
KV = 2
GROUP = HEADS // KV
HD = 128
BT = 64
CAP = 2
PAGES = 154
HOME = PAGES - CAP * (N_INST - 1)
OTHERB = 4
MAXB = 48
LOW = -1e30
SCALE = math.log2(math.e) / math.sqrt(HD)
NEAR = (1, 7, 2, 6, 3, 5, 4)


def iota(shape, dim):
    return lax.broadcasted_iota(jnp.int32, shape, dim)


def dot(a, b):
    return jnp.dot(a, b, preferred_element_type=F32)


def dot_t(a, b):
    return lax.dot_general(a, b, (((1,), (1,)), ((), ())), preferred_element_type=F32)


def remote(src, dst, send, recv, where):
    return pltpu.make_async_remote_copy(
        src_ref=src, dst_ref=dst, send_sem=send, recv_sem=recv, device_id=where, device_id_type=MESH
    )


def drain(ref, sem):
    pltpu.make_async_copy(ref, ref, sem).wait()


def kernel(
    q_ref, k_hbm, v_hbm, tab_ref, ctx_ref, w_hbm, out_ref,
    kbuf, vbuf, wbuf, qall, meta, abuf, rsend, rrecv, a2, a2f, tsh, own, ysend, yrecv,
    ld, qs, qr, ms, mr, zs, zr, xs, xr, cs, cr, rs, rr, gs, gr, ys, yr,
):
    me = lax.axis_index("inst")
    tp = lax.axis_index("tp")
    z, xc = me // 8, me % 8
    x, c = xc // 2, xc % 2

    barrier = pltpu.get_barrier_semaphore()

    def greet(d, carry):
        pl.semaphore_signal(barrier, inc=1, device_id={"inst": (me + d) % N_INST}, device_id_type=MESH)
        return carry

    lax.fori_loop(1, N_INST, greet, 0)
    for d in range(1, TP):
        pl.semaphore_signal(barrier, inc=1, device_id={"tp": (tp + d) % TP}, device_id_type=MESH)

    half = HEADS * HD // 2
    loads = [
        pltpu.make_async_copy(k_hbm.at[pl.ds(0, HOME)], kbuf.at[pl.ds(0, HOME)], ld.at[0]),
        pltpu.make_async_copy(v_hbm.at[pl.ds(0, HOME)], vbuf.at[pl.ds(0, HOME)], ld.at[1]),
        pltpu.make_async_copy(k_hbm.at[pl.ds(HOME, PAGES - HOME)], kbuf.at[pl.ds(HOME, PAGES - HOME)], ld.at[2]),
        pltpu.make_async_copy(v_hbm.at[pl.ds(HOME, PAGES - HOME)], vbuf.at[pl.ds(HOME, PAGES - HOME)], ld.at[3]),
        pltpu.make_async_copy(w_hbm.at[pl.ds(0, half)], wbuf.at[0], ld.at[4]),
        pltpu.make_async_copy(w_hbm.at[pl.ds(half, half)], wbuf.at[1], ld.at[5]),
    ]
    for copy in loads:
        copy.start()

    tab = tab_ref[...]
    row8, lane8 = iota((R, 128), 0), iota((R, 128), 1)
    ctx = jnp.zeros((R, 1), jnp.int32)
    for n in range(R):
        ctx = jnp.where(iota((R, 1), 0) == n, ctx_ref[n], ctx)
    lender, slot = lane8 >> 1, lane8 & 1
    target = lender * PAGES + HOME + (((lender - me) & (N_INST - 1)) - 1) * CAP + slot
    target = jnp.where(lender == me, -5, target)
    slots = jnp.zeros((R, 128), jnp.int32)
    home = jnp.zeros((R, 128), jnp.int32)
    for b in range(MAXB):
        valid = jnp.clip(ctx - b * BT, 0, BT)
        page = tab[:, b : b + 1]
        slots = slots + jnp.where(page == target, valid, 0)
        if b < OTHERB:
            home = home + jnp.where(page == me * PAGES + lane8, valid, 0)
    longest = jnp.sum(jnp.where(ctx > OTHERB * BT, iota((R, 1), 0), 0).astype(F32), axis=0, keepdims=True)
    slots = jnp.sum(slots.astype(F32), axis=0, keepdims=True)
    slots = jnp.where(lane8[0:1] == 2 * me, longest, slots)
    meta[me] = slots.astype(jnp.int32)
    q = q_ref[...]
    pick = iota((HEADS, 128), 1).astype(F32) == longest * HEADS + iota((HEADS, 128), 0).astype(F32)
    qall[me] = dot(pick.astype(F32).astype(BF16), q).astype(BF16)

    pl.semaphore_wait(barrier, N_INST - 1 + TP - 1)

    def send_q(dest, dz):
        remote(qall.at[me], qall.at[me], qs, qr.at[dz], {"inst": dest}).start()
        remote(meta.at[me], meta.at[me], ms, mr.at[dz], {"inst": dest}).start()

    def near(i):
        step = (i + 1) // 2
        return (step * (1 - 2 * ((i + 1) % 2))) & (ZN - 1)

    for e in range(1, 8):
        send_q(z * 8 + ((xc + e) & 7), 0)

    def send_qs(i, carry):
        dz = near(i)
        for e in range(8):
            send_q(((z + dz) & 7) * 8 + e, dz)
        return carry

    lax.fori_loop(1, ZN, send_qs, 0)

    prow, plane = iota((128, 128), 0), iota((128, 128), 1)
    perm = plane == (prow & 7) * HEADS + (prow >> 6) * GROUP + ((prow >> 3) & 7)
    qp = dot(perm.astype(F32).astype(BF16), q).astype(BF16)
    tokens = HOME * BT
    spread = (iota((128, tokens), 1) >> 6) == iota((128, tokens), 0)
    vtok = dot(home.astype(F32).astype(BF16), spread.astype(F32).astype(BF16))
    bias = jnp.where((iota((R, tokens), 1) & (BT - 1)).astype(F32) < vtok, 0.0, LOW)
    loads[0].wait()
    loads[1].wait()
    short = iota((R, 1), 0).astype(F32) != longest
    outs = []
    for k in range(KV):
        keys = kbuf[pl.ds(0, HOME), k].reshape(tokens, HD)
        values = vbuf[pl.ds(0, HOME), k].reshape(tokens, HD)
        s = dot_t(qp[k * 64 : (k + 1) * 64], keys).reshape(GROUP, R, tokens) * SCALE + bias[None]
        top = jnp.max(s, axis=-1, keepdims=True)
        p = jnp.exp2(s - top)
        total = jnp.sum(p, axis=-1, keepdims=True)
        o = dot(p.reshape(64, tokens).astype(BF16), values).reshape(GROUP, R, HD)
        outs.append(jnp.where(short[None], o / total, 0.0))
    for g in range(GROUP):
        abuf[me, :, g * HD : (g + 1) * HD] = jnp.concatenate([outs[0][g], outs[1][g]], axis=0).astype(BF16)

    zc = {}
    for d in NEAR:
        zc[d] = remote(abuf.at[me], abuf.at[me], zs.at[d], zr.at[d], {"inst": ((z + d) & 7) * 8 + xc})
        zc[d].start()

    kv_of = (iota((HEADS, 256), 1) >> 6) & 1
    kv_bias = jnp.where(kv_of == iota((HEADS, 256), 0) // GROUP, 0.0, LOW)
    lane256 = iota((8, 256), 1)
    lane16 = iota((HEADS, 128), 1)
    loads[2].wait()
    loads[3].wait()

    def lend(zh):
        rows = meta[pl.ds(zh * 8, 8)].reshape(8, 128)
        v = [jnp.sum(jnp.where(lane8 == 2 * me + s, rows, 0).astype(F32), axis=-1, keepdims=True) for s in range(CAP)]
        limit = jnp.where(lane256 < 128, v[0], v[1])
        bias8 = jnp.where((lane256 & (BT - 1)).astype(F32) < limit, 0.0, LOW)
        pages = [HOME - CAP + CAP * ((me - (zh * 8 + i)) & (N_INST - 1)) for i in range(8)]
        ss = [
            dot_t(qall[zh * 8 + i], kbuf[pl.ds(pages[i], CAP)].reshape(256, HD)) * SCALE
            + (bias8[i : i + 1] + kv_bias)
            for i in range(8)
        ]
        for i in range(8):
            top = jnp.maximum(jnp.max(ss[i], axis=-1, keepdims=True), -1e20).astype(BF16).astype(F32)
            p = jnp.exp2(ss[i] - top)
            total = jnp.sum(p, axis=-1, keepdims=True)
            o = dot(p.astype(BF16), vbuf[pl.ds(pages[i], CAP)].reshape(256, HD))
            high = total.astype(BF16).astype(F32)
            stats = jnp.where(lane16 < 64, top, jnp.where(lane16 < 96, high, total - high))
            rsend[zh * 8 + i, 0:16] = o.astype(BF16)
            rsend[zh * 8 + i, 16:32] = stats.astype(BF16)

    def send_r(h):
        remote(rsend.at[h], rrecv.at[me], rs, rr, {"inst": h}).start()

    drain(qall.at[pl.ds(0, 7)], qr.at[0])
    drain(meta.at[pl.ds(0, 7)], mr.at[0])
    lend(z)
    for e in range(1, 8):
        send_r(z * 8 + ((xc + e) & 7))

    def lend_z(i, carry):
        dz = near(i)
        drain(qall.at[pl.ds(0, 8)], qr.at[dz])
        drain(meta.at[pl.ds(0, 8)], mr.at[dz])
        zh = (z - dz) & 7
        lend(zh)
        for e in range(8):
            send_r(zh * 8 + e)
        return carry

    lax.fori_loop(1, ZN, lend_z, 0)

    xcopies = []

    def along_x(zz, k):
        for d in range(1, XN):
            block = abuf.at[zz * 8 + xc]
            copy = remote(block, block, xs.at[4 * k + d], xr.at[4 * k + d], {"inst": z * 8 + ((x + d) & 3) * 2 + c})
            copy.start()
            xcopies.append((d, copy))

    along_x(z, 0)
    for d in NEAR:
        zc[d].wait_recv()
        along_x((z - d) & 7, d)

    rrecv[me, 0:16] = jnp.zeros((HEADS, HD), BF16)
    rrecv[me, 16:32] = jnp.where(lane16 < 64, -1e20, 0.0).astype(BF16)
    drain(rrecv.at[pl.ds(0, N_INST - 1)], rr)

    def tops(i, best):
        for e in range(8):
            best = jnp.maximum(best, rrecv[i * 8 + e, 16:32].astype(F32))
        return best

    best = lax.fori_loop(0, 8, tops, jnp.full((HEADS, HD), -1e20, F32))
    best = jnp.broadcast_to(best[:, 0:1], (HEADS, HD))

    def merge(i, carry):
        num, den = carry
        for e in range(8):
            stats = rrecv[i * 8 + e, 16:32].astype(F32)
            f = jnp.exp2(jnp.broadcast_to(stats[:, 0:1], (HEADS, HD)) - best)
            num = num + f * rrecv[i * 8 + e, 0:16].astype(F32)
            den = den + f * stats
        return num, den

    zero = jnp.zeros((HEADS, HD), F32)
    num, den = lax.fori_loop(0, 8, merge, (zero, zero))
    a2[me] = (num / (den[:, 64:65] + den[:, 96:97])).astype(BF16)

    def send_a2(d, carry):
        remote(a2.at[me], a2.at[me], gs, gr, {"inst": (me + d) % N_INST}).start()
        return carry

    lax.fori_loop(1, N_INST, send_a2, 0)

    sib = {"inst": me + 1 - 2 * c}
    ccopies = []

    def across(xx, k):
        for zz in range(ZN):
            block = abuf.at[zz * 8 + xx * 2 + c]
            copy = remote(block, block, cs.at[zz * 4 + k], cr.at[zz * 4 + k], sib)
            copy.start()
            ccopies.append(copy)

    across(x, 0)
    for dd in (1, 3, 2):
        for d, copy in xcopies:
            if d == dd:
                copy.wait_recv()
        across((x - dd) & 3, dd)
    for copy in ccopies:
        copy.wait_recv()

    loads[4].wait()
    loads[5].wait()

    def project(i, carry):
        a = abuf[pl.ds(i * 16, 16)].reshape(256, half)
        t0 = dot(a, wbuf[0]).reshape(16, 16, HD)
        t1 = dot(a, wbuf[1]).reshape(16, 16, HD)
        tsh[pl.ds(i * 16, 16)] = t0[:, 0:8] + t1[:, 8:16]
        return carry

    lax.fori_loop(0, 4, project, 0)

    owners = meta[...].reshape(N_INST, 128)
    mine = iota((N_INST, 128), 1) == 2 * iota((N_INST, 128), 0)
    own[...] = jnp.broadcast_to(
        jnp.sum(jnp.where(mine, owners, 0).astype(F32), axis=-1, keepdims=True), (N_INST, 128)
    )
    drain(a2.at[pl.ds(0, N_INST - 1)], gr)
    a2f[...] = a2[...].astype(F32).reshape(N_INST * HEADS, HD)
    left = [a2f[pl.ds(h, N_INST, stride=HEADS), :].astype(BF16) for h in range(HEADS)]
    t2 = dot(jnp.concatenate(left[:8], axis=1), wbuf[0]) + dot(jnp.concatenate(left[8:], axis=1), wbuf[1])
    frow = row8.astype(F32)
    for i in range(N_INST):
        t = tsh[i] + jnp.where(frow == own[i : i + 1, :], t2[i : i + 1, :], 0.0)
        ysend[i // 16, (i % 16) * 8 : (i % 16) * 8 + 8, :] = t
    ycopies = []
    for d in range(1, TP):
        to = (tp + d) % TP
        copy = remote(ysend.at[to], yrecv.at[d], ys.at[d], yr.at[d], {"tp": to})
        copy.start()
        ycopies.append(copy)
    for copy in ycopies:
        copy.wait_recv()
    out_ref[...] = (ysend[tp] + yrecv[1] + yrecv[2] + yrecv[3]).astype(BF16)

    for copy in ycopies + ccopies + [copy for _, copy in xcopies] + list(zc.values()):
        copy.wait_send()
    drain(qall.at[pl.ds(0, N_INST - 1)], qs)
    drain(meta.at[pl.ds(0, N_INST - 1)], ms)
    drain(rsend.at[pl.ds(0, N_INST - 1)], rs)
    drain(a2.at[pl.ds(0, N_INST - 1)], gs)


def local(queries, keys_cache, value_block_cache, block_table, ctx_len, out_weight):
    dma = pltpu.SemaphoreType.DMA
    vmem = pl.BlockSpec(memory_space=pltpu.VMEM)
    hbm = pl.BlockSpec(memory_space=pl.ANY)
    smem = pl.BlockSpec(memory_space=pltpu.SMEM)
    return pl.pallas_call(
        kernel,
        out_shape=jax.ShapeDtypeStruct((N_INST * R // TP, HD), BF16),
        in_specs=[vmem, hbm, hbm, vmem, smem, hbm],
        out_specs=vmem,
        scratch_shapes=[
            pltpu.VMEM((PAGES, KV, BT, HD), BF16),
            pltpu.VMEM((PAGES, KV, BT, HD), BF16),
            pltpu.VMEM((2, HEADS * HD // 2, HD), BF16),
            pltpu.VMEM((N_INST, HEADS, HD), BF16),
            pltpu.VMEM((N_INST, 1, 128), jnp.int32),
            pltpu.VMEM((N_INST, HEADS, GROUP * HD), BF16),
            pltpu.VMEM((N_INST, 32, HD), BF16),
            pltpu.VMEM((N_INST, 32, HD), BF16),
            pltpu.VMEM((N_INST, HEADS, HD), BF16),
            pltpu.VMEM((N_INST * HEADS, HD), F32),
            pltpu.VMEM((N_INST, R, HD), F32),
            pltpu.VMEM((N_INST, 128), F32),
            pltpu.VMEM((TP, N_INST * R // TP, HD), F32),
            pltpu.VMEM((TP, N_INST * R // TP, HD), F32),
            dma((6,)),
            dma, dma((ZN,)), dma, dma((ZN,)),
            dma((ZN,)), dma((ZN,)),
            dma((4 * ZN,)), dma((4 * ZN,)),
            dma((4 * ZN,)), dma((4 * ZN,)),
            dma, dma,
            dma, dma,
            dma((TP,)), dma((TP,)),
        ],
        name="paged_decode",
        compiler_params=pltpu.CompilerParams(
            collective_id=0, has_side_effects=True, vmem_limit_bytes=48 * 2**20
        ),
    )(
        queries.reshape(R * HEADS, HD), keys_cache, value_block_cache, block_table, ctx_len, out_weight
    )


def solution(mesh):
    return jax.shard_map(
        local,
        mesh=mesh,
        in_specs=(
            P("inst", "tp", None),
            P("inst", "tp", None, None),
            P("inst", "tp", None, None),
            P("inst", None),
            P("inst"),
            P("tp", "inst"),
        ),
        out_specs=P("tp", "inst"),
        check_vma=False,
    )
```

```python
import math

import jax
import jax.numpy as jnp
from jax import lax
from jax.experimental import pallas as pl
from jax.experimental.pallas import tpu as pltpu
from jax.sharding import PartitionSpec as P

MESH = pl.DeviceIdType.MESH
F32 = jnp.float32
BF16 = jnp.bfloat16

N_INST = 64
TP = 4
ZN, XN = 8, 4
R = 8
HEADS = 16
KV = 2
GROUP = HEADS // KV
HD = 128
BT = 64
CAP = 2
PAGES = 154
HOME = PAGES - CAP * (N_INST - 1)
OTHERB = 4
MAXB = 48
LOW = -1e30
SCALE = math.log2(math.e) / math.sqrt(HD)
ORDER = (0, 1, 7, 2, 6, 3, 5, 4)
NEAR = ORDER[1:]
BATCHES = ((1, 2), (3, 2), (5, 3))


def iota(shape, dim):
    return lax.broadcasted_iota(jnp.int32, shape, dim)


def dot(a, b):
    return jnp.dot(a, b, preferred_element_type=F32)


def dot_t(a, b):
    return lax.dot_general(a, b, (((1,), (1,)), ((), ())), preferred_element_type=F32)


def remote(src, dst, send, recv, where):
    return pltpu.make_async_remote_copy(
        src_ref=src, dst_ref=dst, send_sem=send, recv_sem=recv, device_id=where, device_id_type=MESH
    )


def drain(ref, sem):
    pltpu.make_async_copy(ref, ref, sem).wait()


def kernel(
    q_hbm, k_hbm, v_hbm, tab_hbm, ctx_hbm, w_hbm, out_ref,
    q_buf, tab_buf, ctx_buf, kbuf, vbuf, wbuf, qall, meta, abuf,
    rsend, rrecv, ssend, srecv, r2send, r2recv, s2send, s2recv,
    a2, a2f, own, ysend, yrecv, y2send, y2recv,
    ld, qs, ms, qr, mr, zqr, zmr, zs, zr, xs, xr, cs, cr, rs, rr, ss, sr, r2s, r2r, s2s, s2r,
    gs, gr, zgr, ys, yr, y2s, y2r,
):
    me = lax.axis_index("inst")
    tp = lax.axis_index("tp")
    z, xc = me // 8, me % 8
    x, c = xc // 2, xc % 2

    barrier = pltpu.get_barrier_semaphore()

    others = [{"inst": ((z + d) & 7) * 8 + xc} for d in NEAR]
    others += [{"inst": z * 8 + ((xc + e) & 7)} for e in range(1, 8)]
    others += [{"tp": (tp + d) % TP} for d in range(1, TP)]
    for where in others:
        pl.semaphore_signal(barrier, inc=1, device_id=where, device_id_type=MESH)

    half = HEADS * HD // 2
    small = [
        pltpu.make_async_copy(ctx_hbm, ctx_buf, ld.at[6]),
        pltpu.make_async_copy(tab_hbm, tab_buf, ld.at[7]),
        pltpu.make_async_copy(q_hbm, q_buf, ld.at[8]),
    ]
    loads = [
        pltpu.make_async_copy(k_hbm.at[pl.ds(0, HOME)], kbuf.at[pl.ds(0, HOME)], ld.at[0]),
        pltpu.make_async_copy(v_hbm.at[pl.ds(0, HOME)], vbuf.at[pl.ds(0, HOME)], ld.at[1]),
        pltpu.make_async_copy(k_hbm.at[pl.ds(HOME, PAGES - HOME)], kbuf.at[pl.ds(HOME, PAGES - HOME)], ld.at[2]),
        pltpu.make_async_copy(v_hbm.at[pl.ds(HOME, PAGES - HOME)], vbuf.at[pl.ds(HOME, PAGES - HOME)], ld.at[3]),
        pltpu.make_async_copy(w_hbm.at[pl.ds(0, half)], wbuf.at[0], ld.at[4]),
        pltpu.make_async_copy(w_hbm.at[pl.ds(half, half)], wbuf.at[1], ld.at[5]),
    ]
    for copy in small + loads:
        copy.start()
    for copy in small:
        copy.wait()

    tab = tab_buf[...]
    row8, lane8 = iota((R, 128), 0), iota((R, 128), 1)
    ctx = jnp.zeros((R, 1), jnp.int32)
    for n in range(R):
        ctx = jnp.where(iota((R, 1), 0) == n, ctx_buf[n], ctx)
    lender, slot = lane8 >> 1, lane8 & 1
    target = lender * PAGES + HOME + (((lender - me) & (N_INST - 1)) - 1) * CAP + slot
    target = jnp.where(lender == me, -5, target)
    slots = jnp.zeros((R, 128), jnp.int32)
    home = jnp.zeros((R, 128), jnp.int32)
    for b in range(MAXB):
        valid = jnp.clip(ctx - b * BT, 0, BT)
        page = tab[:, b : b + 1]
        slots = slots + jnp.where(page == target, valid, 0)
        if b < OTHERB:
            home = home + jnp.where(page == me * PAGES + lane8, valid, 0)
    longest = jnp.sum(jnp.where(ctx > OTHERB * BT, iota((R, 1), 0), 0).astype(F32), axis=0, keepdims=True)
    slots = jnp.sum(slots.astype(F32), axis=0, keepdims=True)
    slots = jnp.where(lane8[0:1] == 2 * me, longest, slots)
    meta[0, xc] = slots.astype(jnp.int32)
    q = q_buf[...]
    pick = iota((HEADS, 128), 1).astype(F32) == longest * HEADS + iota((HEADS, 128), 0).astype(F32)
    qall[0, xc] = dot(pick.astype(F32).astype(BF16), q).astype(BF16)

    prow, plane = iota((128, 128), 0), iota((128, 128), 1)
    perm = plane == (prow & 7) * HEADS + (prow >> 6) * GROUP + ((prow >> 3) & 7)
    qp = dot(perm.astype(F32).astype(BF16), q).astype(BF16)
    tokens = HOME * BT
    spread = (iota((128, tokens), 1) >> 6) == iota((128, tokens), 0)
    vtok = dot(home.astype(F32).astype(BF16), spread.astype(F32).astype(BF16))
    bias = jnp.where((iota((R, tokens), 1) & (BT - 1)).astype(F32) < vtok, 0.0, LOW)
    loads[0].wait()
    loads[1].wait()
    short = iota((R, 1), 0).astype(F32) != longest
    outs = []
    for k in range(KV):
        keys = kbuf[pl.ds(0, HOME), k].reshape(tokens, HD)
        values = vbuf[pl.ds(0, HOME), k].reshape(tokens, HD)
        s = dot_t(qp[k * 64 : (k + 1) * 64], keys).reshape(GROUP, R, tokens) * SCALE + bias[None]
        top = jnp.max(s, axis=-1, keepdims=True)
        p = jnp.exp2(s - top)
        total = jnp.sum(p, axis=-1, keepdims=True)
        o = dot(p.reshape(64, tokens).astype(BF16), values).reshape(GROUP, R, HD)
        outs.append(jnp.where(short[None], o / total, 0.0))
    for g in range(GROUP):
        abuf[me, :, g * HD : (g + 1) * HD] = jnp.concatenate([outs[0][g], outs[1][g]], axis=0).astype(BF16)

    pl.semaphore_wait(barrier, len(others))

    def along_z(ref, send, recv):
        for i in (7, 5, 6, 3, 4, 1, 2):
            remote(ref.at[0, xc], ref.at[i, xc], send, recv.at[i], {"inst": ((z + ORDER[i]) & 7) * 8 + xc}).start()

    def around(ref, first, count, send, recv):
        block = ref.at[pl.ds(first, count), xc]
        for e in range(1, 8):
            remote(block, block, send, recv, {"inst": z * 8 + ((xc + e) & 7)}).start()

    def relay_q(batch):
        first, count = BATCHES[batch]
        for i in range(first, first + count):
            drain(qall.at[0, 0], zqr.at[i])
            drain(meta.at[0, 0], zmr.at[i])
        around(qall, first, count, qs, qr.at[batch])
        around(meta, first, count, ms, mr.at[batch])

    along_z(qall, qs, zqr)
    along_z(meta, ms, zmr)
    around(qall, 0, 1, qs, qr.at[3])
    around(meta, 0, 1, ms, mr.at[3])

    sib = {"inst": me + 1 - 2 * c}
    copies = {}

    def pass_z(dz, step):
        block = abuf.at[((z - dz) & 7) * 8 + xc]
        slot = (dz + step) & 7
        copies["z", slot] = remote(block, block, zs.at[slot], zr.at[slot], {"inst": ((z + step) & 7) * 8 + xc})
        copies["z", slot].start()

    def take(kind, *key):
        copies[(kind,) + key].wait_recv()

    def pass_x(dz, dx, step):
        block = abuf.at[((z - dz) & 7) * 8 + ((x - dx) & 3) * 2 + c]
        to = (dx + step) & 3
        slot = 4 * dz + to
        copies["x", dz, to] = remote(
            block, block, xs.at[slot], xr.at[slot], {"inst": z * 8 + ((x + step) & 3) * 2 + c}
        )
        copies["x", dz, to].start()

    def across(dz, dx):
        block = abuf.at[((z - dz) & 7) * 8 + ((x - dx) & 3) * 2 + c]
        slot = 4 * dz + dx
        copies["c", dz, dx] = remote(block, block, cs.at[slot], cr.at[slot], sib)
        copies["c", dz, dx].start()

    def start_x(*dzs):
        for dz in dzs:
            pass_x(dz, 0, 1)
            pass_x(dz, 0, -1)
            across(dz, 0)

    def relay_x(*dzs):
        for dz in dzs:
            take("x", dz, 1)
            take("x", dz, 3)
            if dz % 2 == 0:
                pass_x(dz, 1, 1)
            else:
                pass_x(dz, 3, -1)
            across(dz, 1)
            across(dz, 3)

    pass_z(0, 1)
    pass_z(0, -1)

    kv_of = (iota((HEADS, 256), 1) >> 6) & 1
    kv_bias = jnp.where(kv_of == iota((HEADS, 256), 0) // GROUP, 0.0, LOW)
    lane256 = iota((8, 256), 1)
    diag = iota((HEADS, 128), 1) == iota((HEADS, 128), 0)
    diag16 = iota((HEADS, 128), 1) == iota((HEADS, 128), 0) + HEADS
    loads[2].wait()
    loads[3].wait()

    def lend(i, zh, out, stats_out):
        rows = meta[i].reshape(8, 128)
        v = [jnp.sum(jnp.where(lane8 == 2 * me + s, rows, 0).astype(F32), axis=-1, keepdims=True) for s in range(CAP)]
        limit = jnp.where(lane256 < 128, v[0], v[1])
        limit = jnp.where(iota((8, 256), 0) == me - zh * 8, 0.0, limit)
        bias8 = jnp.where((lane256 & (BT - 1)).astype(F32) < limit, 0.0, LOW)
        pages = [HOME - CAP + CAP * ((me - (zh * 8 + e)) & (N_INST - 1)) for e in range(8)]
        scores = [
            dot_t(qall[i, e], kbuf[pl.ds(pages[e], CAP)].reshape(256, HD)) * SCALE
            + (bias8[e : e + 1] + kv_bias)
            for e in range(8)
        ]
        for e in range(8):
            top = jnp.maximum(jnp.max(scores[e], axis=-1, keepdims=True), -1e20)
            p = jnp.exp2(scores[e] - top)
            total = jnp.sum(p, axis=-1, keepdims=True)
            o = dot(p.astype(BF16), vbuf[pl.ds(pages[e], CAP)].reshape(256, HD))
            stats = jnp.where(diag, top, jnp.where(diag16, total, 0.0))
            stats_out[i, e] = jnp.sum(stats, axis=0, keepdims=True)
            out[i, e] = o.astype(BF16)

    def near(i):
        step = (i + 1) // 2
        return (step * (1 - 2 * ((i + 1) % 2))) & (ZN - 1)

    def lend_z(i, carry):
        zh = (z - near(i)) & 7
        lend(i, zh, rsend, ssend)
        remote(rsend.at[i], rrecv.at[i], rs, rr, {"inst": zh * 8 + xc}).start()
        remote(ssend.at[i], srecv.at[i], ss, sr, {"inst": zh * 8 + xc}).start()
        return carry

    def wait_q(batch):
        first, count = BATCHES[batch]
        drain(qall.at[pl.ds(0, count), pl.ds(0, 7)], qr.at[batch])
        drain(meta.at[pl.ds(0, count), pl.ds(0, 7)], mr.at[batch])

    relay_q(0)
    relay_q(1)
    take("z", 1)
    pass_z(1, 1)
    take("z", 7)
    pass_z(7, -1)
    drain(qall.at[0, pl.ds(0, 7)], qr.at[3])
    drain(meta.at[0, pl.ds(0, 7)], mr.at[3])
    lend(0, z, rrecv, srecv)
    relay_q(2)
    start_x(0, 1, 7)
    take("z", 2)
    pass_z(2, 1)
    take("z", 6)
    pass_z(6, -1)
    for batch, (first, count) in enumerate(BATCHES):
        wait_q(batch)
        lax.fori_loop(first, first + count, lend_z, 0)
        if batch == 0:
            take("z", 3)
            pass_z(3, 1)
            start_x(2, 6)
    take("z", 5)
    start_x(3, 5)
    take("z", 4)
    start_x(4)
    relay_x(0, 1, 7, 2, 6)

    lanes = iota((1, 128), 1)
    drain(srecv.at[pl.ds(0, 7)], sr)
    stats = srecv[...].reshape(8, 8, 128)
    best = jnp.max(stats, axis=0)
    share = jnp.exp2(stats - best[None])
    den = jnp.sum(share * pltpu.roll(stats.reshape(64, 128), 128 - HEADS, 1).reshape(8, 8, 128), axis=0)
    totals = pltpu.roll(den, HEADS, 1)
    share = jnp.concatenate([share.reshape(64, 128), jnp.zeros((64, 128), F32)], axis=0).T[:HEADS]
    merged = jnp.where(lanes < HEADS, best, jnp.where(lanes < 2 * HEADS, totals, 0.0))
    for e in range(8):
        s2send[e] = merged[e : e + 1]
    drain(rrecv.at[pl.ds(0, 7)], rr)
    for e in range(8):
        terms = [share[:, i * 8 + e : i * 8 + e + 1] * rrecv[i, e].astype(F32) for i in range(8)]
        r2send[e] = (((terms[0] + terms[1]) + (terms[2] + terms[3])) + ((terms[4] + terms[5]) + (terms[6] + terms[7]))).astype(BF16)
    for e in range(1, 8):
        to = (xc + e) & 7
        remote(s2send.at[to], s2recv.at[e], s2s, s2r, {"inst": z * 8 + to}).start()
        remote(r2send.at[to], r2recv.at[e], r2s, r2r, {"inst": z * 8 + to}).start()
    relay_x(3, 5, 4)
    s2recv[0] = s2send[xc]
    r2recv[0] = r2send[xc]
    drain(s2recv.at[pl.ds(0, 7)], s2r)
    stats = s2recv[...].reshape(8, 128)
    share = jnp.exp2(stats - jnp.max(stats, axis=0, keepdims=True))
    den = jnp.sum(share * pltpu.roll(stats, 128 - HEADS, 1), axis=0, keepdims=True)
    share = share / jnp.where(lanes < HEADS, den, 1.0)
    share = jnp.concatenate([share, jnp.zeros((120, 128), F32)], axis=0).T[:HEADS]
    drain(r2recv.at[pl.ds(0, 7)], r2r)
    terms = [share[:, i : i + 1] * r2recv[i].astype(F32) for i in range(8)]
    a2[0, xc] = (((terms[0] + terms[1]) + (terms[2] + terms[3])) + ((terms[4] + terms[5]) + (terms[6] + terms[7]))).astype(BF16)

    along_z(a2, gs, zgr)
    around(a2, 0, 1, gs, gr.at[3])

    def relay_a2(batch):
        first, count = BATCHES[batch]
        for i in range(first, first + count):
            drain(a2.at[0, 0], zgr.at[i])
        around(a2, first, count, gs, gr.at[batch])

    for dz in ORDER:
        take("x", dz, 2)
        across(dz, 2)
    loads[4].wait()
    loads[5].wait()
    for dz in ORDER:
        for dx in range(XN):
            take("c", dz, dx)

    def project(i, carry):
        a = abuf[pl.ds(i * 16, 16)].reshape(256, half)
        t0 = dot(a, wbuf[0]).reshape(16, 16, HD)
        t1 = dot(a, wbuf[1]).reshape(16, 16, HD)
        ysend[i] = (t0[:, 0:8] + t1[:, 8:16]).reshape(128, HD)
        return carry

    lax.fori_loop(0, TP, project, 0)
    ycopies = []
    for d in range(1, TP):
        to = (tp + d) % TP
        ycopies.append(remote(ysend.at[to], yrecv.at[d], ys.at[d], yr.at[d], {"tp": to}))
        ycopies[-1].start()

    relay_a2(0)
    relay_a2(1)
    relay_a2(2)

    for i in range(8):
        zh = (z - ORDER[i]) & 7
        mine = lane8 == 2 * (zh * 8 + row8)
        owner = jnp.sum(jnp.where(mine, meta[i].reshape(8, 128), 0).astype(F32), axis=-1, keepdims=True)
        own[zh] = jnp.broadcast_to(owner, (8, 128))
    drain(a2.at[0, pl.ds(0, 7)], gr.at[3])
    for batch, (first, count) in enumerate(BATCHES):
        drain(a2.at[pl.ds(0, count), pl.ds(0, 7)], gr.at[batch])
    a2f[...] = a2[...].astype(F32).reshape(N_INST * HEADS, HD)
    left = [a2f[pl.ds(h, N_INST, stride=HEADS), :].astype(BF16) for h in range(HEADS)]
    t2 = dot(jnp.concatenate(left[:8], axis=1), wbuf[0]) + dot(jnp.concatenate(left[8:], axis=1), wbuf[1])
    for i in range(8):
        y2send[(z - ORDER[i]) & 7] = t2[i * 8 : i * 8 + 8]
    for d in range(1, TP):
        to = (tp + d) % TP
        ycopies.append(remote(y2send.at[pl.ds(2 * to, 2)], y2recv.at[d], y2s.at[d], y2r.at[d], {"tp": to}))
        ycopies[-1].start()
    for copy in ycopies:
        copy.wait_recv()
    long = (y2send[pl.ds(2 * tp, 2)] + y2recv[1] + y2recv[2] + y2recv[3]).reshape(16, 128)
    frow = row8.astype(F32)
    owner = own[pl.ds(2 * tp, 2)].reshape(16, 128)
    added = [jnp.where(frow == owner[i : i + 1], long[i : i + 1], 0.0) for i in range(N_INST // TP)]
    out_ref[...] = (ysend[tp] + yrecv[1] + yrecv[2] + yrecv[3] + jnp.concatenate(added, axis=0)).astype(BF16)

    for copy in ycopies + list(copies.values()):
        copy.wait_send()
    for ref, sem in ((qall, qs), (meta, ms), (a2, gs)):
        drain(ref.at[pl.ds(0, 7)], sem)
        drain(ref.at[0, pl.ds(0, 7)], sem)
    for ref, sem in ((rsend, rs), (ssend, ss), (r2send, r2s), (s2send, s2s)):
        drain(ref.at[pl.ds(0, 7)], sem)


def local(queries, keys_cache, value_block_cache, block_table, ctx_len, out_weight):
    dma = pltpu.SemaphoreType.DMA
    vmem = pl.BlockSpec(memory_space=pltpu.VMEM)
    hbm = pl.BlockSpec(memory_space=pltpu.HBM)
    return pl.pallas_call(
        kernel,
        out_shape=jax.ShapeDtypeStruct((N_INST * R // TP, HD), BF16),
        in_specs=[hbm] * 6,
        out_specs=vmem,
        scratch_shapes=[
            pltpu.VMEM((R * HEADS, HD), BF16),
            pltpu.VMEM((R, MAXB), jnp.int32),
            pltpu.SMEM((R,), jnp.int32),
            pltpu.VMEM((PAGES, KV, BT, HD), BF16),
            pltpu.VMEM((PAGES, KV, BT, HD), BF16),
            pltpu.VMEM((2, HEADS * HD // 2, HD), BF16),
            pltpu.VMEM((8, 8, HEADS, HD), BF16),
            pltpu.VMEM((8, 8, 1, 128), jnp.int32),
            pltpu.VMEM((N_INST, HEADS, GROUP * HD), BF16),
            pltpu.VMEM((8, 8, HEADS, HD), BF16),
            pltpu.VMEM((8, 8, HEADS, HD), BF16),
            pltpu.VMEM((8, 8, 1, 128), F32),
            pltpu.VMEM((8, 8, 1, 128), F32),
            pltpu.VMEM((8, HEADS, HD), BF16),
            pltpu.VMEM((8, HEADS, HD), BF16),
            pltpu.VMEM((8, 1, 128), F32),
            pltpu.VMEM((8, 1, 128), F32),
            pltpu.VMEM((8, 8, HEADS, HD), BF16),
            pltpu.VMEM((N_INST * HEADS, HD), F32),
            pltpu.VMEM((8, 8, 128), F32),
            pltpu.VMEM((TP, N_INST * R // TP, HD), F32),
            pltpu.VMEM((TP, N_INST * R // TP, HD), F32),
            pltpu.VMEM((8, 8, HD), F32),
            pltpu.VMEM((TP, 2, 8, HD), F32),
            dma((9,)),
            dma, dma, dma((4,)), dma((4,)), dma((ZN,)), dma((ZN,)),
            dma((ZN,)), dma((ZN,)),
            dma((4 * ZN,)), dma((4 * ZN,)),
            dma((4 * ZN,)), dma((4 * ZN,)),
            dma, dma, dma, dma,
            dma, dma, dma, dma,
            dma, dma((4,)), dma((ZN,)),
            dma((TP,)), dma((TP,)),
            dma((TP,)), dma((TP,)),
        ],
        name="paged_decode",
        compiler_params=pltpu.CompilerParams(
            collective_id=0, has_side_effects=True, vmem_limit_bytes=60 * 2**20
        ),
    )(
        queries.reshape(R * HEADS, HD), keys_cache, value_block_cache, block_table, ctx_len, out_weight
    )


def solution(mesh):
    return jax.shard_map(
        local,
        mesh=mesh,
        in_specs=(
            P("inst", "tp", None),
            P("inst", "tp", None, None),
            P("inst", "tp", None, None),
            P("inst", None),
            P("inst"),
            P("tp", "inst"),
        ),
        out_specs=P("tp", "inst"),
        check_vma=False,
    )
```

```python
import math

import jax
import jax.numpy as jnp
from jax import lax
from jax.experimental import pallas as pl
from jax.experimental.pallas import tpu as pltpu
from jax.sharding import PartitionSpec as P

MESH = pl.DeviceIdType.MESH
F32 = jnp.float32
BF16 = jnp.bfloat16

N_INST = 64
TP = 4
ZN, XN = 8, 4
R = 8
HEADS = 16
KV = 2
GROUP = HEADS // KV
HD = 128
BT = 64
CAP = 2
PAGES = 154
HOME = PAGES - CAP * (N_INST - 1)
OTHERB = 4
MAXB = 48
LOW = -1e30
SCALE = math.log2(math.e) / math.sqrt(HD)
ORDER = (0, 1, 7, 2, 6, 4, 3, 5)
NEAR = ORDER[1:]
FAR = sorted(
    ((i, dx, dc) for i in range(8) for dx in range(4) for dc in range(2) if (i, dx, dc) != (0, 0, 0)),
    key=lambda t: -(min(ORDER[t[0]], 8 - ORDER[t[0]]) + min(t[1], 4 - t[1]) + t[2]),
)
AROUND = ((2, 1), (2, 0), (1, 1), (3, 1), (1, 0), (3, 0), (0, 1), (0, 0))
BATCHES = ((1, 2), (3, 2), (5, 3))


def iota(shape, dim):
    return lax.broadcasted_iota(jnp.int32, shape, dim)


def dot(a, b):
    return jnp.dot(a, b, preferred_element_type=F32)


def dot_t(a, b):
    return lax.dot_general(a, b, (((1,), (1,)), ((), ())), preferred_element_type=F32)


def remote(src, dst, send, recv, where):
    return pltpu.make_async_remote_copy(
        src_ref=src, dst_ref=dst, send_sem=send, recv_sem=recv, device_id=where, device_id_type=MESH
    )


def drain(ref, sem):
    pltpu.make_async_copy(ref, ref, sem).wait()


def kernel(
    q_hbm, k_hbm, v_hbm, tab_hbm, ctx_hbm, w_hbm, out_ref,
    q_buf, tab_buf, ctx_buf, kbuf, vbuf, wbuf, qall, meta, abuf,
    rsend, rrecv, ssend, srecv,
    a2, a2f, own, ysend, yrecv, y2send, y2recv,
    ld, qs, ms, qr, mr, zqr, zmr, zs, zr, xs, xr, cs, cr, rs, rr, ss, sr,
    gs, gr, ys, yr, y2s, y2r,
):
    me = lax.axis_index("inst")
    tp = lax.axis_index("tp")
    z, xc = me // 8, me % 8
    x, c = xc // 2, xc % 2

    small = [
        pltpu.make_async_copy(ctx_hbm, ctx_buf, ld.at[6]),
        pltpu.make_async_copy(tab_hbm, tab_buf, ld.at[7]),
        pltpu.make_async_copy(q_hbm, q_buf, ld.at[8]),
    ]
    for copy in small:
        copy.start()

    barrier = pltpu.get_barrier_semaphore()

    others = [{"inst": ((z + d) & 7) * 8 + xc} for d in NEAR]
    others += [{"inst": z * 8 + ((xc + e) & 7)} for e in range(1, 8)]
    others += [{"tp": (tp + d) % TP} for d in range(1, TP)]
    for where in others:
        pl.semaphore_signal(barrier, inc=1, device_id=where, device_id_type=MESH)

    half = HEADS * HD // 2
    loads = [
        pltpu.make_async_copy(k_hbm.at[pl.ds(0, HOME)], kbuf.at[pl.ds(0, HOME)], ld.at[0]),
        pltpu.make_async_copy(v_hbm.at[pl.ds(0, HOME)], vbuf.at[pl.ds(0, HOME)], ld.at[1]),
        pltpu.make_async_copy(k_hbm.at[pl.ds(HOME, PAGES - HOME)], kbuf.at[pl.ds(HOME, PAGES - HOME)], ld.at[2]),
        pltpu.make_async_copy(v_hbm.at[pl.ds(HOME, PAGES - HOME)], vbuf.at[pl.ds(HOME, PAGES - HOME)], ld.at[3]),
        pltpu.make_async_copy(w_hbm.at[pl.ds(0, half)], wbuf.at[0], ld.at[4]),
        pltpu.make_async_copy(w_hbm.at[pl.ds(half, half)], wbuf.at[1], ld.at[5]),
    ]
    for copy in loads:
        copy.start()
    for copy in small:
        copy.wait()

    tab = tab_buf[...]
    row8, lane8 = iota((R, 128), 0), iota((R, 128), 1)
    ctx = jnp.zeros((R, 1), jnp.int32)
    for n in range(R):
        ctx = jnp.where(iota((R, 1), 0) == n, ctx_buf[n], ctx)
    lender, slot = lane8 >> 1, lane8 & 1
    target = lender * PAGES + HOME + (((lender - me) & (N_INST - 1)) - 1) * CAP + slot
    target = jnp.where(lender == me, -5, target)
    slots = jnp.zeros((R, 128), jnp.int32)
    home = jnp.zeros((R, 128), jnp.int32)
    for b in range(MAXB):
        valid = jnp.clip(ctx - b * BT, 0, BT)
        page = tab[:, b : b + 1]
        slots = slots + jnp.where(page == target, valid, 0)
        if b < OTHERB:
            home = home + jnp.where(page == me * PAGES + lane8, valid, 0)
    longest = jnp.sum(jnp.where(ctx > OTHERB * BT, iota((R, 1), 0), 0).astype(F32), axis=0, keepdims=True)
    slots = jnp.sum(slots.astype(F32), axis=0, keepdims=True)
    slots = jnp.where(lane8[0:1] == 2 * me, longest, slots)
    meta[0, xc] = slots.astype(jnp.int32)
    q = q_buf[...]
    pick = iota((HEADS, 128), 1).astype(F32) == longest * HEADS + iota((HEADS, 128), 0).astype(F32)
    qall[0, xc] = dot(pick.astype(F32).astype(BF16), q).astype(BF16)

    pl.semaphore_wait(barrier, len(others))

    def along_z(ref, send, recv):
        for i in (5, 6, 7, 3, 4, 1, 2):
            remote(ref.at[0, xc], ref.at[i, xc], send, recv.at[i], {"inst": ((z + ORDER[i]) & 7) * 8 + xc}).start()

    def around(ref, first, count, send, recv):
        block = ref.at[pl.ds(first, count), xc]
        for e in range(1, 8):
            remote(block, block, send, recv, {"inst": z * 8 + ((xc + e) & 7)}).start()

    def relay_q(batch):
        first, count = BATCHES[batch]
        for i in range(first, first + count):
            drain(qall.at[0, 0], zqr.at[i])
            drain(meta.at[0, 0], zmr.at[i])
        around(qall, first, count, qs, qr.at[batch])
        around(meta, first, count, ms, mr.at[batch])

    along_z(qall, qs, zqr)
    along_z(meta, ms, zmr)
    around(qall, 0, 1, qs, qr.at[3])
    around(meta, 0, 1, ms, mr.at[3])

    sib = {"inst": me + 1 - 2 * c}
    copies = {}

    def pass_z(dz, step):
        block = abuf.at[((z - dz) & 7) * 8 + xc]
        slot = (dz + step) & 7
        copies["z", slot] = remote(block, block, zs.at[slot], zr.at[slot], {"inst": ((z + step) & 7) * 8 + xc})
        copies["z", slot].start()

    def take(kind, *key):
        copies[(kind,) + key].wait_recv()

    def pass_x(dz, dx, step):
        block = abuf.at[((z - dz) & 7) * 8 + ((x - dx) & 3) * 2 + c]
        to = (dx + step) & 3
        slot = 4 * dz + to
        copies["x", dz, to] = remote(
            block, block, xs.at[slot], xr.at[slot], {"inst": z * 8 + ((x + step) & 3) * 2 + c}
        )
        copies["x", dz, to].start()

    def across(dz, dx):
        block = abuf.at[((z - dz) & 7) * 8 + ((x - dx) & 3) * 2 + c]
        slot = 4 * dz + dx
        copies["c", dz, dx] = remote(block, block, cs.at[slot], cr.at[slot], sib)
        copies["c", dz, dx].start()

    def start_x(*dzs):
        for dz in dzs:
            pass_x(dz, 0, 1)
            pass_x(dz, 0, -1)
            across(dz, 0)

    def relay_x(*dzs):
        for dz in dzs:
            take("x", dz, 1)
            take("x", dz, 3)
            if dz % 2 == 0:
                pass_x(dz, 1, 1)
            else:
                pass_x(dz, 3, -1)
            across(dz, 1)
            across(dz, 3)

    prow, plane = iota((128, 128), 0), iota((128, 128), 1)
    perm = plane == (prow & 7) * HEADS + (prow >> 6) * GROUP + ((prow >> 3) & 7)
    qp = dot(perm.astype(F32).astype(BF16), q).astype(BF16)
    tokens = HOME * BT
    spread = (iota((128, tokens), 1) >> 6) == iota((128, tokens), 0)
    vtok = dot(home.astype(F32).astype(BF16), spread.astype(F32).astype(BF16))
    bias = jnp.where((iota((R, tokens), 1) & (BT - 1)).astype(F32) < vtok, 0.0, LOW)
    loads[0].wait()
    loads[1].wait()
    short = iota((R, 1), 0).astype(F32) != longest
    outs = []
    for k in range(KV):
        keys = kbuf[pl.ds(0, HOME), k].reshape(tokens, HD)
        values = vbuf[pl.ds(0, HOME), k].reshape(tokens, HD)
        s = dot_t(qp[k * 64 : (k + 1) * 64], keys).reshape(GROUP, R, tokens) * SCALE + bias[None]
        top = jnp.max(s, axis=-1, keepdims=True)
        p = jnp.exp2(s - top)
        total = jnp.sum(p, axis=-1, keepdims=True)
        o = dot(p.reshape(64, tokens).astype(BF16), values).reshape(GROUP, R, HD)
        outs.append(jnp.where(short[None], o / total, 0.0))
    for g in range(GROUP):
        abuf[me, :, g * HD : (g + 1) * HD] = jnp.concatenate([outs[0][g], outs[1][g]], axis=0).astype(BF16)

    pass_z(0, 1)
    pass_z(0, -1)

    kv_of = (iota((HEADS, 256), 1) >> 6) & 1
    kv_bias = jnp.where(kv_of == iota((HEADS, 256), 0) // GROUP, 0.0, LOW)
    lane256 = iota((8, 256), 1)
    diag = iota((HEADS, 128), 1) == iota((HEADS, 128), 0)
    diag16 = iota((HEADS, 128), 1) == iota((HEADS, 128), 0) + HEADS
    loads[2].wait()
    loads[3].wait()

    def lend(i, zh):
        rows = meta[i].reshape(8, 128)
        v = [jnp.sum(jnp.where(lane8 == 2 * me + s, rows, 0).astype(F32), axis=-1, keepdims=True) for s in range(CAP)]
        limit = jnp.where(lane256 < 128, v[0], v[1])
        limit = jnp.where(iota((8, 256), 0) == me - zh * 8, 0.0, limit)
        bias8 = jnp.where((lane256 & (BT - 1)).astype(F32) < limit, 0.0, LOW)
        pages = [HOME - CAP + CAP * ((me - (zh * 8 + e)) & (N_INST - 1)) for e in range(8)]
        scores = [
            dot_t(qall[i, e], kbuf[pl.ds(pages[e], CAP)].reshape(256, HD)) * SCALE
            + (bias8[e : e + 1] + kv_bias)
            for e in range(8)
        ]
        for e in range(8):
            top = jnp.maximum(jnp.max(scores[e], axis=-1, keepdims=True), -1e20)
            p = jnp.exp2(scores[e] - top)
            total = jnp.sum(p, axis=-1, keepdims=True)
            o = dot(p.astype(BF16), vbuf[pl.ds(pages[e], CAP)].reshape(256, HD))
            stats = jnp.where(diag, top, jnp.where(diag16, total, 0.0))
            ssend[i, e] = jnp.sum(stats, axis=0, keepdims=True)
            rsend[i, e] = o.astype(BF16)

    def near(i):
        step = (i + 1) // 2
        return jnp.where(i < 5, (step * (1 - 2 * ((i + 1) % 2))) & (ZN - 1), jnp.where(i == 5, 4, jnp.where(i == 6, 3, 5)))

    def send_r(i, zh):
        for dx, dc in AROUND:
            e = ((x + dx) & 3) * 2 + (c ^ dc)
            to = {"inst": zh * 8 + e}
            remote(ssend.at[i, e], srecv.at[i, xc], ss, sr.at[i], to).start()
            remote(rsend.at[i, e], rrecv.at[i, xc], rs, rr.at[i], to).start()

    def lend_z(i, carry):
        zh = (z - near(i)) & 7
        lend(i, zh)
        send_r(i, zh)
        return carry

    def wait_q(batch):
        first, count = BATCHES[batch]
        drain(qall.at[pl.ds(0, count), pl.ds(0, 7)], qr.at[batch])
        drain(meta.at[pl.ds(0, count), pl.ds(0, 7)], mr.at[batch])

    relay_q(0)
    relay_q(1)
    take("z", 1)
    pass_z(1, 1)
    take("z", 7)
    pass_z(7, -1)
    drain(qall.at[0, pl.ds(0, 7)], qr.at[3])
    drain(meta.at[0, pl.ds(0, 7)], mr.at[3])
    lend(0, z)
    for dx, dc in AROUND[:-1]:
        e = ((x + dx) & 3) * 2 + (c ^ dc)
        remote(ssend.at[0, e], srecv.at[0, xc], ss, sr.at[0], {"inst": z * 8 + e}).start()
        remote(rsend.at[0, e], rrecv.at[0, xc], rs, rr.at[0], {"inst": z * 8 + e}).start()
    srecv[0, xc] = ssend[0, xc]
    rrecv[0, xc] = rsend[0, xc]
    relay_q(2)
    start_x(0, 1, 7)
    take("z", 2)
    pass_z(2, 1)
    take("z", 6)
    pass_z(6, -1)
    for batch, (first, count) in enumerate(BATCHES):
        wait_q(batch)
        lax.fori_loop(first, first + count, lend_z, 0)
        if batch == 0:
            take("z", 3)
            pass_z(3, 1)
            start_x(2, 6)
    take("z", 5)
    start_x(3, 5)
    take("z", 4)
    start_x(4)
    relay_x(0, 1, 7, 2, 6)

    relay_x(3, 5, 4)

    lanes = iota((1, 128), 1)
    for ref, sem in ((srecv, sr), (rrecv, rr)):
        drain(ref.at[0, pl.ds(0, 7)], sem.at[0])
        for i in range(1, 8):
            drain(ref.at[i], sem.at[i])
    stats = srecv[...].reshape(64, 128)
    share = jnp.exp2(stats - jnp.max(stats, axis=0, keepdims=True))
    den = jnp.sum(share * pltpu.roll(stats, 128 - HEADS, 1), axis=0, keepdims=True)
    share = share / jnp.where(lanes < HEADS, den, 1.0)
    share = jnp.concatenate([share, jnp.zeros((64, 128), F32)], axis=0).T[:HEADS]
    parts = []
    for i in range(8):
        terms = [share[:, i * 8 + e : i * 8 + e + 1] * rrecv[i, e].astype(F32) for e in range(8)]
        parts.append(sum(terms[1:], terms[0]))
    a2[0, xc] = sum(parts[1:], parts[0]).astype(BF16)

    for i, dx, dc in FAR:
        to = ((z + ORDER[i]) & 7) * 8 + ((x + dx) & 3) * 2 + (c ^ dc)
        remote(a2.at[0, xc], a2.at[i, xc], gs, gr.at[i], {"inst": to}).start()

    for dz in ORDER:
        take("x", dz, 2)
        across(dz, 2)
    loads[4].wait()
    loads[5].wait()
    for dz in ORDER:
        for dx in range(XN):
            take("c", dz, dx)

    def project(i, carry):
        a = abuf[pl.ds(i * 16, 16)].reshape(256, half)
        t0 = dot(a, wbuf[0]).reshape(16, 16, HD)
        t1 = dot(a, wbuf[1]).reshape(16, 16, HD)
        ysend[i] = (t0[:, 0:8] + t1[:, 8:16]).reshape(128, HD)
        return carry

    lax.fori_loop(0, TP, project, 0)
    ycopies = []
    for d in range(1, TP):
        to = (tp + d) % TP
        ycopies.append(remote(ysend.at[to], yrecv.at[d], ys.at[d], yr.at[d], {"tp": to}))
        ycopies[-1].start()


    for i in range(8):
        zh = (z - ORDER[i]) & 7
        mine = lane8 == 2 * (zh * 8 + row8)
        owner = jnp.sum(jnp.where(mine, meta[i].reshape(8, 128), 0).astype(F32), axis=-1, keepdims=True)
        own[zh] = jnp.broadcast_to(owner, (8, 128))
    drain(a2.at[0, pl.ds(0, 7)], gr.at[0])
    for i in range(1, 8):
        drain(a2.at[i], gr.at[i])
    a2f[...] = a2[...].astype(F32).reshape(N_INST * HEADS, HD)
    left = [a2f[pl.ds(h, N_INST, stride=HEADS), :].astype(BF16) for h in range(HEADS)]
    t2 = dot(jnp.concatenate(left[:8], axis=1), wbuf[0]) + dot(jnp.concatenate(left[8:], axis=1), wbuf[1])
    for i in range(8):
        y2send[(z - ORDER[i]) & 7] = t2[i * 8 : i * 8 + 8]
    for d in range(1, TP):
        to = (tp + d) % TP
        ycopies.append(remote(y2send.at[pl.ds(2 * to, 2)], y2recv.at[d], y2s.at[d], y2r.at[d], {"tp": to}))
        ycopies[-1].start()
    for copy in ycopies:
        copy.wait_recv()
    long = (y2send[pl.ds(2 * tp, 2)] + y2recv[1] + y2recv[2] + y2recv[3]).reshape(16, 128)
    frow = row8.astype(F32)
    owner = own[pl.ds(2 * tp, 2)].reshape(16, 128)
    added = [jnp.where(frow == owner[i : i + 1], long[i : i + 1], 0.0) for i in range(N_INST // TP)]
    out_ref[...] = (ysend[tp] + yrecv[1] + yrecv[2] + yrecv[3] + jnp.concatenate(added, axis=0)).astype(BF16)

    for copy in ycopies + list(copies.values()):
        copy.wait_send()
    for ref, sem in ((qall, qs), (meta, ms), (rsend, rs), (ssend, ss), (a2, gs)):
        drain(ref.at[pl.ds(0, 7)], sem)
        drain(ref.at[0, pl.ds(0, 7)], sem)


def local(queries, keys_cache, value_block_cache, block_table, ctx_len, out_weight):
    dma = pltpu.SemaphoreType.DMA
    vmem = pl.BlockSpec(memory_space=pltpu.VMEM)
    hbm = pl.BlockSpec(memory_space=pltpu.HBM)
    return pl.pallas_call(
        kernel,
        out_shape=pltpu.VMEM((N_INST * R // TP, HD), BF16),
        in_specs=[hbm] * 6,
        out_specs=vmem,
        scratch_shapes=[
            pltpu.VMEM((R * HEADS, HD), BF16),
            pltpu.VMEM((R, MAXB), jnp.int32),
            pltpu.SMEM((R,), jnp.int32),
            pltpu.VMEM((PAGES, KV, BT, HD), BF16),
            pltpu.VMEM((PAGES, KV, BT, HD), BF16),
            pltpu.VMEM((2, HEADS * HD // 2, HD), BF16),
            pltpu.VMEM((8, 8, HEADS, HD), BF16),
            pltpu.VMEM((8, 8, 1, 128), jnp.int32),
            pltpu.VMEM((N_INST, HEADS, GROUP * HD), BF16),
            pltpu.VMEM((8, 8, HEADS, HD), BF16),
            pltpu.VMEM((8, 8, HEADS, HD), BF16),
            pltpu.VMEM((8, 8, 1, 128), F32),
            pltpu.VMEM((8, 8, 1, 128), F32),
            pltpu.VMEM((8, 8, HEADS, HD), BF16),
            pltpu.VMEM((N_INST * HEADS, HD), F32),
            pltpu.VMEM((8, 8, 128), F32),
            pltpu.VMEM((TP, N_INST * R // TP, HD), F32),
            pltpu.VMEM((TP, N_INST * R // TP, HD), F32),
            pltpu.VMEM((8, 8, HD), F32),
            pltpu.VMEM((TP, 2, 8, HD), F32),
            dma((9,)),
            dma, dma, dma((4,)), dma((4,)), dma((ZN,)), dma((ZN,)),
            dma((ZN,)), dma((ZN,)),
            dma((4 * ZN,)), dma((4 * ZN,)),
            dma((4 * ZN,)), dma((4 * ZN,)),
            dma, dma((ZN,)), dma, dma((ZN,)),
            dma, dma((ZN,)),
            dma((TP,)), dma((TP,)),
            dma((TP,)), dma((TP,)),
        ],
        name="paged_decode",
        compiler_params=pltpu.CompilerParams(
            collective_id=0, has_side_effects=True, vmem_limit_bytes=60 * 2**20
        ),
    )(
        queries.reshape(R * HEADS, HD), keys_cache, value_block_cache, block_table, ctx_len, out_weight
    )


def solution(mesh):
    return jax.shard_map(
        local,
        mesh=mesh,
        in_specs=(
            P("inst", "tp", None),
            P("inst", "tp", None, None),
            P("inst", "tp", None, None),
            P("inst", None),
            P("inst"),
            P("tp", "inst"),
        ),
        out_specs=P("tp", "inst"),
        check_vma=False,
    )
```

```python
import math

import jax
import jax.numpy as jnp
from jax import lax
from jax.experimental import pallas as pl
from jax.experimental.pallas import tpu as pltpu
from jax.sharding import PartitionSpec as P

MESH = pl.DeviceIdType.MESH
F32 = jnp.float32
BF16 = jnp.bfloat16

N_INST = 64
TP = 4
ZN, XN = 8, 4
R = 8
HEADS = 16
KV = 2
GROUP = HEADS // KV
HD = 128
BT = 64
CAP = 2
PAGES = 154
HOME = PAGES - CAP * (N_INST - 1)
OTHERB = 4
MAXB = 48
LOW = -1e30
SCALE = math.log2(math.e) / math.sqrt(HD)
ORDER = (0, 1, 7, 2, 6, 4, 3, 5)
NEAR = ORDER[1:]
FAR = sorted(
    ((i, dx, dc) for i in range(8) for dx in range(4) for dc in range(2) if (i, dx, dc) != (0, 0, 0)),
    key=lambda t: -(min(ORDER[t[0]], 8 - ORDER[t[0]]) + min(t[1], 4 - t[1]) + t[2]),
)
AROUND = ((2, 1), (2, 0), (1, 1), (3, 1), (1, 0), (3, 0), (0, 1), (0, 0))


def iota(shape, dim):
    return lax.broadcasted_iota(jnp.int32, shape, dim)


def dot(a, b):
    return jnp.dot(a, b, preferred_element_type=F32)


def dot_t(a, b):
    return lax.dot_general(a, b, (((1,), (1,)), ((), ())), preferred_element_type=F32)


def remote(src, dst, send, recv, where):
    return pltpu.make_async_remote_copy(
        src_ref=src, dst_ref=dst, send_sem=send, recv_sem=recv, device_id=where, device_id_type=MESH
    )


def drain(ref, sem):
    pltpu.make_async_copy(ref, ref, sem).wait()


def kernel(
    q_hbm, k_hbm, v_hbm, tab_hbm, ctx_hbm, w_hbm, out_ref,
    q_buf, tab_buf, ctx_buf, qpb, outs, kbuf, vbuf, wbuf, qall, meta, abuf,
    rsend, rrecv, ssend, srecv,
    a2, a2f, own, ysend, yrecv, y2send, y2recv,
    ld, qs, ms, qr, mr, zqr, zmr, zs, zr, xs, xr, cs, cr, rs, rr, ss, sr,
    gs, gr, ys, yr, y2s, y2r,
):
    me = lax.axis_index("inst")
    tp = lax.axis_index("tp")
    z, xc = me // 8, me % 8
    x, c = xc // 2, xc % 2

    small = [
        pltpu.make_async_copy(ctx_hbm, ctx_buf, ld.at[6]),
        pltpu.make_async_copy(tab_hbm, tab_buf, ld.at[7]),
        pltpu.make_async_copy(q_hbm, q_buf, ld.at[8]),
    ]
    for copy in small:
        copy.start()

    barrier = pltpu.get_barrier_semaphore()

    others = [{"inst": ((z + d) & 7) * 8 + xc} for d in NEAR]
    others += [{"inst": z * 8 + ((xc + e) & 7)} for e in range(1, 8)]
    others += [{"tp": (tp + d) % TP} for d in range(1, TP)]
    for where in others:
        pl.semaphore_signal(barrier, inc=1, device_id=where, device_id_type=MESH)

    half = HEADS * HD // 2
    loads = [
        pltpu.make_async_copy(k_hbm.at[pl.ds(0, HOME)], kbuf.at[pl.ds(0, HOME)], ld.at[0]),
        pltpu.make_async_copy(v_hbm.at[pl.ds(0, HOME)], vbuf.at[pl.ds(0, HOME)], ld.at[1]),
        pltpu.make_async_copy(k_hbm.at[pl.ds(HOME, PAGES - HOME)], kbuf.at[pl.ds(HOME, PAGES - HOME)], ld.at[2]),
        pltpu.make_async_copy(v_hbm.at[pl.ds(HOME, PAGES - HOME)], vbuf.at[pl.ds(HOME, PAGES - HOME)], ld.at[3]),
        pltpu.make_async_copy(w_hbm.at[pl.ds(0, half)], wbuf.at[0], ld.at[4]),
        pltpu.make_async_copy(w_hbm.at[pl.ds(half, half)], wbuf.at[1], ld.at[5]),
    ]
    for copy in loads:
        copy.start()
    for copy in small:
        copy.wait()

    tab = tab_buf[...]
    row8, lane8 = iota((R, 128), 0), iota((R, 128), 1)
    ctx = jnp.zeros((R, 1), jnp.int32)
    for n in range(R):
        ctx = jnp.where(iota((R, 1), 0) == n, ctx_buf[n], ctx)
    lender, slot = lane8 >> 1, lane8 & 1
    target = lender * PAGES + HOME + (((lender - me) & (N_INST - 1)) - 1) * CAP + slot
    target = jnp.where(lender == me, -5, target)
    slots = jnp.zeros((R, 128), jnp.int32)
    home = jnp.zeros((R, 128), jnp.int32)
    for b in range(MAXB):
        valid = jnp.clip(ctx - b * BT, 0, BT)
        page = tab[:, b : b + 1]
        slots = slots + jnp.where(page == target, valid, 0)
        if b < OTHERB:
            home = home + jnp.where(page == me * PAGES + lane8, valid, 0)
    longest = jnp.sum(jnp.where(ctx > OTHERB * BT, iota((R, 1), 0), 0).astype(F32), axis=0, keepdims=True)
    slots = jnp.sum(slots.astype(F32), axis=0, keepdims=True)
    slots = jnp.where(lane8[0:1] == 2 * me, longest, slots)
    meta[0, xc] = slots.astype(jnp.int32)
    q = q_buf[...]
    pick = iota((HEADS, 128), 1).astype(F32) == longest * HEADS + iota((HEADS, 128), 0).astype(F32)
    qall[0, xc] = dot(pick.astype(F32).astype(BF16), q).astype(BF16)

    prow, plane = iota((128, 128), 0), iota((128, 128), 1)
    perm = plane == (prow & 7) * HEADS + (prow >> 6) * GROUP + ((prow >> 3) & 7)
    qp = dot(perm.astype(F32).astype(BF16), q).astype(BF16)
    tokens = HOME * BT
    spread = (iota((128, tokens), 1) >> 6) == iota((128, tokens), 0)
    vtok = dot(home.astype(F32).astype(BF16), spread.astype(F32).astype(BF16))
    bias = jnp.where((iota((R, tokens), 1) & (BT - 1)).astype(F32) < vtok, 0.0, LOW)
    loads[0].wait()
    loads[1].wait()
    short = iota((R, 1), 0).astype(F32) != longest
    qpb[...] = qp

    def own_blocks(k, carry):
        keys = kbuf[pl.ds(0, HOME), k].reshape(tokens, HD)
        values = vbuf[pl.ds(0, HOME), k].reshape(tokens, HD)
        s = dot_t(qpb[pl.ds(pl.multiple_of(k * 64, 64), 64)], keys).reshape(GROUP, R, tokens) * SCALE + bias[None]
        top = jnp.max(s, axis=-1, keepdims=True)
        p = jnp.exp2(s - top)
        total = jnp.sum(p, axis=-1, keepdims=True)
        o = dot(p.reshape(64, tokens).astype(BF16), values).reshape(GROUP, R, HD)
        outs[k] = jnp.where(short[None], o / total, 0.0)
        return carry

    lax.fori_loop(0, KV, own_blocks, 0)
    for g in range(GROUP):
        abuf[me, :, g * HD : (g + 1) * HD] = jnp.concatenate([outs[0, g], outs[1, g]], axis=0).astype(BF16)

    pl.semaphore_wait(barrier, len(others))

    def along_z(ref, send, recv):
        for i in (5, 6, 7, 3, 4, 1, 2):
            remote(ref.at[0, xc], ref.at[i, xc], send, recv.at[i], {"inst": ((z + ORDER[i]) & 7) * 8 + xc}).start()

    def around(ref, i, send, recv):
        block = ref.at[i, xc]
        for e in range(1, 8):
            remote(block, block, send, recv, {"inst": z * 8 + ((xc + e) & 7)}).start()

    def relay_q(i, carry):
        drain(qall.at[0, 0], zqr.at[i])
        drain(meta.at[0, 0], zmr.at[i])
        around(qall, i, qs, qr.at[i])
        around(meta, i, ms, mr.at[i])
        return carry

    along_z(qall, qs, zqr)
    along_z(meta, ms, zmr)
    around(qall, 0, qs, qr.at[0])
    around(meta, 0, ms, mr.at[0])

    sib = {"inst": me + 1 - 2 * c}
    copies = {}

    def pass_z(dz, step):
        block = abuf.at[((z - dz) & 7) * 8 + xc]
        slot = (dz + step) & 7
        copies["z", slot] = remote(block, block, zs.at[slot], zr.at[slot], {"inst": ((z + step) & 7) * 8 + xc})
        copies["z", slot].start()

    def take(kind, *key):
        copies[(kind,) + key].wait_recv()

    def pass_x(dz, dx, step):
        block = abuf.at[((z - dz) & 7) * 8 + ((x - dx) & 3) * 2 + c]
        to = (dx + step) & 3
        slot = 4 * dz + to
        copies["x", dz, to] = remote(
            block, block, xs.at[slot], xr.at[slot], {"inst": z * 8 + ((x + step) & 3) * 2 + c}
        )
        copies["x", dz, to].start()

    def across(dz, dx):
        block = abuf.at[((z - dz) & 7) * 8 + ((x - dx) & 3) * 2 + c]
        slot = 4 * dz + dx
        copies["c", dz, dx] = remote(block, block, cs.at[slot], cr.at[slot], sib)
        copies["c", dz, dx].start()

    def start_x(*dzs):
        for dz in dzs:
            pass_x(dz, 0, 1)
            pass_x(dz, 0, -1)
            across(dz, 0)

    def relay_x(*dzs):
        for dz in dzs:
            take("x", dz, 1)
            take("x", dz, 3)
            if dz % 2 == 0:
                pass_x(dz, 1, 1)
            else:
                pass_x(dz, 3, -1)
            across(dz, 1)
            across(dz, 3)

    pass_z(0, 1)
    pass_z(0, -1)

    kv_of = (iota((HEADS, 256), 1) >> 6) & 1
    kv_bias = jnp.where(kv_of == iota((HEADS, 256), 0) // GROUP, 0.0, LOW)
    lane256 = iota((8, 256), 1)
    diag = iota((HEADS, 128), 1) == iota((HEADS, 128), 0)
    diag16 = iota((HEADS, 128), 1) == iota((HEADS, 128), 0) + HEADS
    loads[2].wait()
    loads[3].wait()

    def lend(i, zh):
        rows = meta[i].reshape(8, 128)
        v = [jnp.sum(jnp.where(lane8 == 2 * me + s, rows, 0).astype(F32), axis=-1, keepdims=True) for s in range(CAP)]
        limit = jnp.where(lane256 < 128, v[0], v[1])
        limit = jnp.where(iota((8, 256), 0) == me - zh * 8, 0.0, limit)
        bias8 = jnp.where((lane256 & (BT - 1)).astype(F32) < limit, 0.0, LOW)
        pages = [HOME - CAP + CAP * ((me - (zh * 8 + e)) & (N_INST - 1)) for e in range(8)]
        scores = [
            dot_t(qall[i, e], kbuf[pl.ds(pages[e], CAP)].reshape(256, HD)) * SCALE
            + (bias8[e : e + 1] + kv_bias)
            for e in range(8)
        ]
        for e in range(8):
            top = jnp.maximum(jnp.max(scores[e], axis=-1, keepdims=True), -1e20)
            p = jnp.exp2(scores[e] - top)
            total = jnp.sum(p, axis=-1, keepdims=True)
            o = dot(p.astype(BF16), vbuf[pl.ds(pages[e], CAP)].reshape(256, HD))
            stats = jnp.where(diag, top, jnp.where(diag16, total, 0.0))
            ssend[i, e] = jnp.sum(stats, axis=0, keepdims=True)
            rsend[i, e] = o.astype(BF16)

    def near(i):
        step = (i + 1) // 2
        return jnp.where(i < 5, (step * (1 - 2 * ((i + 1) % 2))) & (ZN - 1), jnp.where(i == 5, 4, jnp.where(i == 6, 3, 5)))

    def send_r(i, zh):
        def one(dx, dc):
            e = ((x + dx) & 3) * 2 + (c ^ dc)
            to = {"inst": zh * 8 + e}
            remote(ssend.at[i, e], srecv.at[i, xc], ss, sr.at[i], to).start()
            remote(rsend.at[i, e], rrecv.at[i, xc], rs, rr.at[i], to).start()

        for dx, dc in AROUND[:-1]:
            one(dx, dc)

        @pl.when(i > 0)
        def _():
            one(0, 0)

    def lend_z(i, carry):
        zh = (z - near(i)) & 7
        drain(qall.at[0, pl.ds(0, 7)], qr.at[i])
        drain(meta.at[0, pl.ds(0, 7)], mr.at[i])
        lend(i, zh)
        send_r(i, zh)
        return carry

    lax.fori_loop(1, 5, relay_q, 0)
    take("z", 1)
    pass_z(1, 1)
    take("z", 7)
    pass_z(7, -1)
    lax.fori_loop(0, 1, lend_z, 0)
    lax.fori_loop(5, 8, relay_q, 0)
    start_x(0, 1, 7)
    take("z", 2)
    pass_z(2, 1)
    take("z", 6)
    pass_z(6, -1)
    lax.fori_loop(1, 3, lend_z, 0)
    take("z", 3)
    pass_z(3, 1)
    start_x(2, 6)
    lax.fori_loop(3, 8, lend_z, 0)
    srecv[0, xc] = ssend[0, xc]
    rrecv[0, xc] = rsend[0, xc]
    take("z", 5)
    start_x(3, 5)
    take("z", 4)
    start_x(4)
    relay_x(0, 1, 7, 2, 6)

    relay_x(3, 5, 4)

    lanes = iota((1, 128), 1)
    for ref, sem in ((srecv, sr), (rrecv, rr)):
        drain(ref.at[0, pl.ds(0, 7)], sem.at[0])
        for i in range(1, 8):
            drain(ref.at[i], sem.at[i])
    stats = srecv[...].reshape(64, 128)
    share = jnp.exp2(stats - jnp.max(stats, axis=0, keepdims=True))
    den = jnp.sum(share * pltpu.roll(stats, 128 - HEADS, 1), axis=0, keepdims=True)
    share = share / jnp.where(lanes < HEADS, den, 1.0)
    share = jnp.concatenate([share, jnp.zeros((64, 128), F32)], axis=0).T[:HEADS]
    parts = []
    for i in range(8):
        terms = [share[:, i * 8 + e : i * 8 + e + 1] * rrecv[i, e].astype(F32) for e in range(8)]
        parts.append(sum(terms[1:], terms[0]))
    a2[0, xc] = sum(parts[1:], parts[0]).astype(BF16)

    for i, dx, dc in FAR:
        to = ((z + ORDER[i]) & 7) * 8 + ((x + dx) & 3) * 2 + (c ^ dc)
        remote(a2.at[0, xc], a2.at[i, xc], gs, gr.at[i], {"inst": to}).start()

    for dz in ORDER:
        take("x", dz, 2)
        across(dz, 2)
    loads[4].wait()
    loads[5].wait()
    for dz in ORDER:
        for dx in range(XN):
            take("c", dz, dx)

    def project(i, carry):
        a = abuf[pl.ds(i * 16, 16)].reshape(256, half)
        t0 = dot(a, wbuf[0]).reshape(16, 16, HD)
        t1 = dot(a, wbuf[1]).reshape(16, 16, HD)
        ysend[i] = (t0[:, 0:8] + t1[:, 8:16]).reshape(128, HD)
        return carry

    lax.fori_loop(0, TP, project, 0)
    ycopies = []
    for d in range(1, TP):
        to = (tp + d) % TP
        ycopies.append(remote(ysend.at[to], yrecv.at[d], ys.at[d], yr.at[d], {"tp": to}))
        ycopies[-1].start()


    for i in range(8):
        zh = (z - ORDER[i]) & 7
        mine = lane8 == 2 * (zh * 8 + row8)
        owner = jnp.sum(jnp.where(mine, meta[i].reshape(8, 128), 0).astype(F32), axis=-1, keepdims=True)
        own[zh] = jnp.broadcast_to(owner, (8, 128))
    for i in (0, 1, 2, 3, 4, 6, 7, 5):
        drain(a2.at[i] if i else a2.at[0, pl.ds(0, 7)], gr.at[i])
        a2f[i * 128 : i * 128 + 128] = a2[i].astype(F32).reshape(128, HD)
    left = [a2f[pl.ds(h, N_INST, stride=HEADS), :].astype(BF16) for h in range(HEADS)]
    t2 = dot(jnp.concatenate(left[:8], axis=1), wbuf[0]) + dot(jnp.concatenate(left[8:], axis=1), wbuf[1])
    for i in range(8):
        y2send[(z - ORDER[i]) & 7] = t2[i * 8 : i * 8 + 8]
    for d in range(1, TP):
        to = (tp + d) % TP
        ycopies.append(remote(y2send.at[pl.ds(2 * to, 2)], y2recv.at[d], y2s.at[d], y2r.at[d], {"tp": to}))
        ycopies[-1].start()
    for copy in list(copies.values()):
        copy.wait_send()
    for ref, sem in ((qall, qs), (meta, ms), (rsend, rs), (ssend, ss), (a2, gs)):
        drain(ref.at[pl.ds(0, 7)], sem)
        drain(ref.at[0, pl.ds(0, 7)], sem)
    for copy in ycopies:
        copy.wait()
    long = (y2send[pl.ds(2 * tp, 2)] + y2recv[1] + y2recv[2] + y2recv[3]).reshape(16, 128)
    frow = row8.astype(F32)
    owner = own[pl.ds(2 * tp, 2)].reshape(16, 128)
    added = [jnp.where(frow == owner[i : i + 1], long[i : i + 1], 0.0) for i in range(N_INST // TP)]
    out_ref[...] = (ysend[tp] + yrecv[1] + yrecv[2] + yrecv[3] + jnp.concatenate(added, axis=0)).astype(BF16)


def local(queries, keys_cache, value_block_cache, block_table, ctx_len, out_weight):
    dma = pltpu.SemaphoreType.DMA
    vmem = pl.BlockSpec(memory_space=pltpu.VMEM)
    hbm = pl.BlockSpec(memory_space=pltpu.HBM)
    return pl.pallas_call(
        kernel,
        out_shape=pltpu.VMEM((N_INST * R // TP, HD), BF16),
        in_specs=[hbm] * 6,
        out_specs=vmem,
        scratch_shapes=[
            pltpu.VMEM((R * HEADS, HD), BF16),
            pltpu.VMEM((R, MAXB), jnp.int32),
            pltpu.SMEM((R,), jnp.int32),
            pltpu.VMEM((R * HEADS, HD), BF16),
            pltpu.VMEM((KV, GROUP, R, HD), F32),
            pltpu.VMEM((PAGES, KV, BT, HD), BF16),
            pltpu.VMEM((PAGES, KV, BT, HD), BF16),
            pltpu.VMEM((2, HEADS * HD // 2, HD), BF16),
            pltpu.VMEM((8, 8, HEADS, HD), BF16),
            pltpu.VMEM((8, 8, 1, 128), jnp.int32),
            pltpu.VMEM((N_INST, HEADS, GROUP * HD), BF16),
            pltpu.VMEM((8, 8, HEADS, HD), BF16),
            pltpu.VMEM((8, 8, HEADS, HD), BF16),
            pltpu.VMEM((8, 8, 1, 128), F32),
            pltpu.VMEM((8, 8, 1, 128), F32),
            pltpu.VMEM((8, 8, HEADS, HD), BF16),
            pltpu.VMEM((N_INST * HEADS, HD), F32),
            pltpu.VMEM((8, 8, 128), F32),
            pltpu.VMEM((TP, N_INST * R // TP, HD), F32),
            pltpu.VMEM((TP, N_INST * R // TP, HD), F32),
            pltpu.VMEM((8, 8, HD), F32),
            pltpu.VMEM((TP, 2, 8, HD), F32),
            dma((9,)),
            dma, dma, dma((ZN,)), dma((ZN,)), dma((ZN,)), dma((ZN,)),
            dma((ZN,)), dma((ZN,)),
            dma((4 * ZN,)), dma((4 * ZN,)),
            dma((4 * ZN,)), dma((4 * ZN,)),
            dma, dma((ZN,)), dma, dma((ZN,)),
            dma, dma((ZN,)),
            dma((TP,)), dma((TP,)),
            dma((TP,)), dma((TP,)),
        ],
        name="paged_decode",
        compiler_params=pltpu.CompilerParams(
            collective_id=0, has_side_effects=True, vmem_limit_bytes=60 * 2**20
        ),
    )(
        queries.reshape(R * HEADS, HD), keys_cache, value_block_cache, block_table, ctx_len, out_weight
    )


def solution(mesh):
    return jax.shard_map(
        local,
        mesh=mesh,
        in_specs=(
            P("inst", "tp", None),
            P("inst", "tp", None, None),
            P("inst", "tp", None, None),
            P("inst", None),
            P("inst"),
            P("tp", "inst"),
        ),
        out_specs=P("tp", "inst"),
        check_vma=False,
    )
```

```python
import math

import jax
import jax.numpy as jnp
from jax import lax
from jax.experimental import pallas as pl
from jax.experimental.pallas import tpu as pltpu
from jax.sharding import PartitionSpec as P

MESH = pl.DeviceIdType.MESH
F32 = jnp.float32
BF16 = jnp.bfloat16

N_INST = 64
TP = 4
ZN, XN = 8, 4
R = 8
HEADS = 16
KV = 2
GROUP = HEADS // KV
HD = 128
BT = 64
CAP = 2
PAGES = 154
HOME = PAGES - CAP * (N_INST - 1)
OTHERB = 4
MAXB = 48
LOW = -1e30
SCALE = math.log2(math.e) / math.sqrt(HD)
ORDER = (0, 1, 7, 2, 6, 4, 3, 5)
NEAR = ORDER[1:]
FAR = sorted(
    ((i, dx, dc) for i in range(8) for dx in range(4) for dc in range(2) if (i, dx, dc) != (0, 0, 0)),
    key=lambda t: -(min(ORDER[t[0]], 8 - ORDER[t[0]]) + min(t[1], 4 - t[1]) + t[2]),
)
AROUND = ((2, 1), (2, 0), (1, 1), (3, 1), (1, 0), (3, 0), (0, 1), (0, 0))


def iota(shape, dim):
    return lax.broadcasted_iota(jnp.int32, shape, dim)


def dot(a, b):
    return jnp.dot(a, b, preferred_element_type=F32)


def dot_t(a, b):
    return lax.dot_general(a, b, (((1,), (1,)), ((), ())), preferred_element_type=F32)


def remote(src, dst, send, recv, where):
    return pltpu.make_async_remote_copy(
        src_ref=src, dst_ref=dst, send_sem=send, recv_sem=recv, device_id=where, device_id_type=MESH
    )


def drain(ref, sem):
    pltpu.make_async_copy(ref, ref, sem).wait()


def kernel(
    q_hbm, k_hbm, v_hbm, tab_hbm, ctx_hbm, w_hbm, out_ref,
    q_buf, tab_buf, ctx_buf, qpb, outs, kbuf, vbuf, wbuf, qall, meta, abuf,
    rsend, rrecv, ssend, srecv,
    a2, a2f, own, ysend, yrecv, y2send, y2recv,
    ld, qs, ms, qr, mr, zqr, zmr, zs, zr, xs, xr, cs, cr, rs, rr, ss, sr,
    gs, gr, ys, yr, y2s, y2r,
):
    me = lax.axis_index("inst")
    tp = lax.axis_index("tp")
    z, xc = me // 8, me % 8
    x, c = xc // 2, xc % 2

    small = [
        pltpu.make_async_copy(ctx_hbm, ctx_buf, ld.at[6]),
        pltpu.make_async_copy(tab_hbm, tab_buf, ld.at[7]),
        pltpu.make_async_copy(q_hbm, q_buf, ld.at[8]),
    ]
    for copy in small:
        copy.start()

    barrier = pltpu.get_barrier_semaphore()

    others = [{"inst": ((z + d) & 7) * 8 + xc} for d in NEAR]
    others += [{"inst": z * 8 + ((xc + e) & 7)} for e in range(1, 8)]
    others += [{"tp": (tp + d) % TP} for d in range(1, TP)]
    for where in others:
        pl.semaphore_signal(barrier, inc=1, device_id=where, device_id_type=MESH)

    half = HEADS * HD // 2
    loads = [
        pltpu.make_async_copy(k_hbm.at[pl.ds(0, HOME)], kbuf.at[pl.ds(0, HOME)], ld.at[0]),
        pltpu.make_async_copy(v_hbm.at[pl.ds(0, HOME)], vbuf.at[pl.ds(0, HOME)], ld.at[1]),
        pltpu.make_async_copy(k_hbm.at[pl.ds(HOME, PAGES - HOME)], kbuf.at[pl.ds(HOME, PAGES - HOME)], ld.at[2]),
        pltpu.make_async_copy(v_hbm.at[pl.ds(HOME, PAGES - HOME)], vbuf.at[pl.ds(HOME, PAGES - HOME)], ld.at[3]),
        pltpu.make_async_copy(w_hbm.at[pl.ds(0, half)], wbuf.at[0], ld.at[4]),
        pltpu.make_async_copy(w_hbm.at[pl.ds(half, half)], wbuf.at[1], ld.at[5]),
    ]
    for copy in loads:
        copy.start()
    for copy in small:
        copy.wait()

    tab = tab_buf[...]
    row8, lane8 = iota((R, 128), 0), iota((R, 128), 1)
    ctx = jnp.zeros((R, 1), jnp.int32)
    for n in range(R):
        ctx = jnp.where(iota((R, 1), 0) == n, ctx_buf[n], ctx)
    lender, slot = lane8 >> 1, lane8 & 1
    target = lender * PAGES + HOME + (((lender - me) & (N_INST - 1)) - 1) * CAP + slot
    target = jnp.where(lender == me, -5, target)
    slots = jnp.zeros((R, 128), jnp.int32)
    home = jnp.zeros((R, 128), jnp.int32)
    for b in range(MAXB):
        valid = jnp.clip(ctx - b * BT, 0, BT)
        page = tab[:, b : b + 1]
        slots = slots + jnp.where(page == target, valid, 0)
        if b < OTHERB:
            home = home + jnp.where(page == me * PAGES + lane8, valid, 0)
    longest = jnp.sum(jnp.where(ctx > OTHERB * BT, iota((R, 1), 0), 0).astype(F32), axis=0, keepdims=True)
    slots = jnp.sum(slots.astype(F32), axis=0, keepdims=True)
    slots = jnp.where(lane8[0:1] == 2 * me, longest, slots)
    meta[0, xc] = slots.astype(jnp.int32)
    q = q_buf[...]
    pick = iota((HEADS, 128), 1).astype(F32) == longest * HEADS + iota((HEADS, 128), 0).astype(F32)
    qall[0, xc] = dot(pick.astype(F32).astype(BF16), q).astype(BF16)

    prow, plane = iota((128, 128), 0), iota((128, 128), 1)
    perm = plane == (prow & 7) * HEADS + (prow >> 6) * GROUP + ((prow >> 3) & 7)
    qp = dot(perm.astype(F32).astype(BF16), q).astype(BF16)
    tokens = HOME * BT
    spread = (iota((128, tokens), 1) >> 6) == iota((128, tokens), 0)
    vtok = dot(home.astype(F32).astype(BF16), spread.astype(F32).astype(BF16))
    bias = jnp.where((iota((R, tokens), 1) & (BT - 1)).astype(F32) < vtok, 0.0, LOW)
    loads[0].wait()
    loads[1].wait()
    short = iota((R, 1), 0).astype(F32) != longest
    qpb[...] = qp

    def own_blocks(k, carry):
        keys = kbuf[pl.ds(0, HOME), k].reshape(tokens, HD)
        values = vbuf[pl.ds(0, HOME), k].reshape(tokens, HD)
        s = dot_t(qpb[pl.ds(pl.multiple_of(k * 64, 64), 64)], keys).reshape(GROUP, R, tokens) * SCALE + bias[None]
        top = jnp.max(s, axis=-1, keepdims=True)
        p = jnp.exp2(s - top)
        total = jnp.sum(p, axis=-1, keepdims=True)
        o = dot(p.reshape(64, tokens).astype(BF16), values).reshape(GROUP, R, HD)
        outs[k] = jnp.where(short[None], o / total, 0.0)
        return carry

    lax.fori_loop(0, KV, own_blocks, 0)
    for g in range(GROUP):
        abuf[me, :, g * HD : (g + 1) * HD] = jnp.concatenate([outs[0, g], outs[1, g]], axis=0).astype(BF16)

    pl.semaphore_wait(barrier, len(others))

    def along_z(ref, send, recv):
        for i in (5, 6, 7, 3, 4, 1, 2):
            remote(ref.at[0, xc], ref.at[i, xc], send, recv.at[i], {"inst": ((z + ORDER[i]) & 7) * 8 + xc}).start()

    def around(ref, i, send, recv):
        block = ref.at[i, xc]
        for e in (4, 5, 3, 2, 6, 7, 1):
            remote(block, block, send, recv, {"inst": z * 8 + ((xc + e) & 7)}).start()

    def relay_q(i, carry):
        drain(qall.at[0, 0], zqr.at[i])
        drain(meta.at[0, 0], zmr.at[i])
        around(qall, i, qs, qr.at[i])
        around(meta, i, ms, mr.at[i])
        return carry

    along_z(qall, qs, zqr)
    along_z(meta, ms, zmr)
    around(qall, 0, qs, qr.at[0])
    around(meta, 0, ms, mr.at[0])

    sib = {"inst": me + 1 - 2 * c}
    copies = {}

    def pass_z(dz, step):
        block = abuf.at[((z - dz) & 7) * 8 + xc]
        slot = (dz + step) & 7
        copies["z", slot] = remote(block, block, zs.at[slot], zr.at[slot], {"inst": ((z + step) & 7) * 8 + xc})
        copies["z", slot].start()

    def take(kind, *key):
        copies[(kind,) + key].wait_recv()

    def pass_x(dz, dx, step):
        block = abuf.at[((z - dz) & 7) * 8 + ((x - dx) & 3) * 2 + c]
        to = (dx + step) & 3
        slot = 4 * dz + to
        copies["x", dz, to] = remote(
            block, block, xs.at[slot], xr.at[slot], {"inst": z * 8 + ((x + step) & 3) * 2 + c}
        )
        copies["x", dz, to].start()

    def across(dz, dx):
        block = abuf.at[((z - dz) & 7) * 8 + ((x - dx) & 3) * 2 + c]
        slot = 4 * dz + dx
        copies["c", dz, dx] = remote(block, block, cs.at[slot], cr.at[slot], sib)
        copies["c", dz, dx].start()

    def start_x(*dzs):
        for dz in dzs:
            pass_x(dz, 0, 1)
            pass_x(dz, 0, -1)
            across(dz, 0)

    def relay_x(*dzs):
        for dz in dzs:
            take("x", dz, 1)
            take("x", dz, 3)
            if dz % 2 == 0:
                pass_x(dz, 1, 1)
            else:
                pass_x(dz, 3, -1)
            across(dz, 1)
            across(dz, 3)

    pass_z(0, 1)
    pass_z(0, -1)

    kv_of = (iota((HEADS, 256), 1) >> 6) & 1
    kv_bias = jnp.where(kv_of == iota((HEADS, 256), 0) // GROUP, 0.0, LOW)
    lane256 = iota((8, 256), 1)
    diag = iota((HEADS, 128), 1) == iota((HEADS, 128), 0)
    diag16 = iota((HEADS, 128), 1) == iota((HEADS, 128), 0) + HEADS
    loads[2].wait()
    loads[3].wait()

    def lend(i, zh):
        rows = meta[i].reshape(8, 128)
        v = [jnp.sum(jnp.where(lane8 == 2 * me + s, rows, 0).astype(F32), axis=-1, keepdims=True) for s in range(CAP)]
        limit = jnp.where(lane256 < 128, v[0], v[1])
        limit = jnp.where(iota((8, 256), 0) == me - zh * 8, 0.0, limit)
        bias8 = jnp.where((lane256 & (BT - 1)).astype(F32) < limit, 0.0, LOW)
        pages = [HOME - CAP + CAP * ((me - (zh * 8 + e)) & (N_INST - 1)) for e in range(8)]
        scores = [
            dot_t(qall[i, e], kbuf[pl.ds(pages[e], CAP)].reshape(256, HD)) * SCALE
            + (bias8[e : e + 1] + kv_bias)
            for e in range(8)
        ]
        for e in range(8):
            top = jnp.maximum(jnp.max(scores[e], axis=-1, keepdims=True), -1e20)
            p = jnp.exp2(scores[e] - top)
            total = jnp.sum(p, axis=-1, keepdims=True)
            o = dot(p.astype(BF16), vbuf[pl.ds(pages[e], CAP)].reshape(256, HD))
            stats = jnp.where(diag, top, jnp.where(diag16, total, 0.0))
            ssend[i, e] = jnp.sum(stats, axis=0, keepdims=True)
            rsend[i, e] = o.astype(BF16)

    def near(i):
        step = (i + 1) // 2
        return jnp.where(i < 5, (step * (1 - 2 * ((i + 1) % 2))) & (ZN - 1), jnp.where(i == 5, 4, jnp.where(i == 6, 3, 5)))

    def send_r(i, zh):
        def one(dx, dc):
            e = ((x + dx) & 3) * 2 + (c ^ dc)
            to = {"inst": zh * 8 + e}
            remote(ssend.at[i, e], srecv.at[i, xc], ss, sr.at[i], to).start()
            remote(rsend.at[i, e], rrecv.at[i, xc], rs, rr.at[i], to).start()

        for dx, dc in AROUND[:-1]:
            one(dx, dc)

        @pl.when(i > 0)
        def _():
            one(0, 0)

    def lend_z(i, carry):
        zh = (z - near(i)) & 7
        drain(qall.at[0, pl.ds(0, 7)], qr.at[i])
        drain(meta.at[0, pl.ds(0, 7)], mr.at[i])
        lend(i, zh)
        send_r(i, zh)
        return carry

    lax.fori_loop(1, 5, relay_q, 0)
    take("z", 1)
    pass_z(1, 1)
    take("z", 7)
    pass_z(7, -1)
    lax.fori_loop(0, 1, lend_z, 0)
    lax.fori_loop(5, 8, relay_q, 0)
    start_x(0, 1, 7)
    take("z", 2)
    pass_z(2, 1)
    take("z", 6)
    pass_z(6, -1)
    lax.fori_loop(1, 3, lend_z, 0)
    take("z", 3)
    pass_z(3, 1)
    start_x(2, 6)
    lax.fori_loop(3, 8, lend_z, 0)
    srecv[0, xc] = ssend[0, xc]
    rrecv[0, xc] = rsend[0, xc]
    take("z", 5)
    start_x(3, 5)
    take("z", 4)
    start_x(4)
    relay_x(0, 1, 7, 2, 6)

    relay_x(3, 5, 4)

    lanes = iota((1, 128), 1)
    for ref, sem in ((srecv, sr), (rrecv, rr)):
        drain(ref.at[0, pl.ds(0, 7)], sem.at[0])
        for i in range(1, 8):
            drain(ref.at[i], sem.at[i])
    stats = srecv[...].reshape(64, 128)
    share = jnp.exp2(stats - jnp.max(stats, axis=0, keepdims=True))
    den = jnp.sum(share * pltpu.roll(stats, 128 - HEADS, 1), axis=0, keepdims=True)
    share = share / jnp.where(lanes < HEADS, den, 1.0)
    share = jnp.concatenate([share, jnp.zeros((64, 128), F32)], axis=0).T[:HEADS]
    parts = []
    for i in range(8):
        terms = [share[:, i * 8 + e : i * 8 + e + 1] * rrecv[i, e].astype(F32) for e in range(8)]
        parts.append(sum(terms[1:], terms[0]))
    a2[0, xc] = sum(parts[1:], parts[0]).astype(BF16)

    for i, dx, dc in FAR:
        to = ((z + ORDER[i]) & 7) * 8 + ((x + dx) & 3) * 2 + (c ^ dc)
        remote(a2.at[0, xc], a2.at[i, xc], gs, gr.at[i], {"inst": to}).start()

    for dz in ORDER:
        take("x", dz, 2)
        across(dz, 2)
    loads[4].wait()
    loads[5].wait()
    for dz in ORDER:
        for dx in range(XN):
            take("c", dz, dx)

    def project(i, carry):
        a = abuf[pl.ds(i * 16, 16)].reshape(256, half)
        t0 = dot(a, wbuf[0]).reshape(16, 16, HD)
        t1 = dot(a, wbuf[1]).reshape(16, 16, HD)
        ysend[i] = (t0[:, 0:8] + t1[:, 8:16]).reshape(128, HD)
        return carry

    lax.fori_loop(0, TP, project, 0)
    ycopies = []
    for d in range(1, TP):
        to = (tp + d) % TP
        ycopies.append(remote(ysend.at[to], yrecv.at[d], ys.at[d], yr.at[d], {"tp": to}))
        ycopies[-1].start()


    for i in range(8):
        zh = (z - ORDER[i]) & 7
        mine = lane8 == 2 * (zh * 8 + row8)
        owner = jnp.sum(jnp.where(mine, meta[i].reshape(8, 128), 0).astype(F32), axis=-1, keepdims=True)
        own[zh] = jnp.broadcast_to(owner, (8, 128))
    for i in (0, 1, 2, 3, 4, 6, 7, 5):
        drain(a2.at[i] if i else a2.at[0, pl.ds(0, 7)], gr.at[i])
        a2f[i * 128 : i * 128 + 128] = a2[i].astype(F32).reshape(128, HD)
    left = [a2f[pl.ds(h, N_INST, stride=HEADS), :].astype(BF16) for h in range(HEADS)]
    t2 = dot(jnp.concatenate(left[:8], axis=1), wbuf[0]) + dot(jnp.concatenate(left[8:], axis=1), wbuf[1])
    for i in range(8):
        y2send[(z - ORDER[i]) & 7] = t2[i * 8 : i * 8 + 8]
    for d in range(1, TP):
        to = (tp + d) % TP
        ycopies.append(remote(y2send.at[pl.ds(2 * to, 2)], y2recv.at[d], y2s.at[d], y2r.at[d], {"tp": to}))
        ycopies[-1].start()
    for copy in list(copies.values()):
        copy.wait_send()
    for ref, sem in ((qall, qs), (meta, ms), (rsend, rs), (ssend, ss), (a2, gs)):
        drain(ref.at[pl.ds(0, 7)], sem)
        drain(ref.at[0, pl.ds(0, 7)], sem)
    for copy in ycopies:
        copy.wait()
    long = (y2send[pl.ds(2 * tp, 2)] + y2recv[1] + y2recv[2] + y2recv[3]).reshape(16, 128)
    frow = row8.astype(F32)
    owner = own[pl.ds(2 * tp, 2)].reshape(16, 128)
    added = [jnp.where(frow == owner[i : i + 1], long[i : i + 1], 0.0) for i in range(N_INST // TP)]
    out_ref[...] = (ysend[tp] + yrecv[1] + yrecv[2] + yrecv[3] + jnp.concatenate(added, axis=0)).astype(BF16)


def local(queries, keys_cache, value_block_cache, block_table, ctx_len, out_weight):
    dma = pltpu.SemaphoreType.DMA
    vmem = pl.BlockSpec(memory_space=pltpu.VMEM)
    hbm = pl.BlockSpec(memory_space=pltpu.HBM)
    return pl.pallas_call(
        kernel,
        out_shape=pltpu.VMEM((N_INST * R // TP, HD), BF16),
        in_specs=[hbm] * 6,
        out_specs=vmem,
        scratch_shapes=[
            pltpu.VMEM((R * HEADS, HD), BF16),
            pltpu.VMEM((R, MAXB), jnp.int32),
            pltpu.SMEM((R,), jnp.int32),
            pltpu.VMEM((R * HEADS, HD), BF16),
            pltpu.VMEM((KV, GROUP, R, HD), F32),
            pltpu.VMEM((PAGES, KV, BT, HD), BF16),
            pltpu.VMEM((PAGES, KV, BT, HD), BF16),
            pltpu.VMEM((2, HEADS * HD // 2, HD), BF16),
            pltpu.VMEM((8, 8, HEADS, HD), BF16),
            pltpu.VMEM((8, 8, 1, 128), jnp.int32),
            pltpu.VMEM((N_INST, HEADS, GROUP * HD), BF16),
            pltpu.VMEM((8, 8, HEADS, HD), BF16),
            pltpu.VMEM((8, 8, HEADS, HD), BF16),
            pltpu.VMEM((8, 8, 1, 128), F32),
            pltpu.VMEM((8, 8, 1, 128), F32),
            pltpu.VMEM((8, 8, HEADS, HD), BF16),
            pltpu.VMEM((N_INST * HEADS, HD), F32),
            pltpu.VMEM((8, 8, 128), F32),
            pltpu.VMEM((TP, N_INST * R // TP, HD), F32),
            pltpu.VMEM((TP, N_INST * R // TP, HD), F32),
            pltpu.VMEM((8, 8, HD), F32),
            pltpu.VMEM((TP, 2, 8, HD), F32),
            dma((9,)),
            dma, dma, dma((ZN,)), dma((ZN,)), dma((ZN,)), dma((ZN,)),
            dma((ZN,)), dma((ZN,)),
            dma((4 * ZN,)), dma((4 * ZN,)),
            dma((4 * ZN,)), dma((4 * ZN,)),
            dma, dma((ZN,)), dma, dma((ZN,)),
            dma, dma((ZN,)),
            dma((TP,)), dma((TP,)),
            dma((TP,)), dma((TP,)),
        ],
        name="paged_decode",
        compiler_params=pltpu.CompilerParams(
            collective_id=0, has_side_effects=True, vmem_limit_bytes=60 * 2**20
        ),
    )(
        queries.reshape(R * HEADS, HD), keys_cache, value_block_cache, block_table, ctx_len, out_weight
    )


def solution(mesh):
    return jax.shard_map(
        local,
        mesh=mesh,
        in_specs=(
            P("inst", "tp", None),
            P("inst", "tp", None, None),
            P("inst", "tp", None, None),
            P("inst", None),
            P("inst"),
            P("tp", "inst"),
        ),
        out_specs=P("tp", "inst"),
        check_vma=False,
    )
```
